512 devices in a mesh: ctx: 64 (over z, y), uly: 8 (over x, core).
Axes of the slice: x: 4, y: 4, z: 16, core: 2. Of those that a mesh axis runs over, the one named last changes fastest.
Arguments:
- queries: bfloat16 [65536, 3584], P(('ctx', 'uly')), may hold values from -10 to 10
- keys: bfloat16 [65536, 3584], P(('ctx', 'uly')), may hold values from -10 to 10
- values: bfloat16 [65536, 3584], P(('ctx', 'uly')), may hold values from -6 to 6
- step_raw: bfloat16 [65536, 56], P(('ctx', 'uly')), may hold values from -4 to 4
- step_bias: float32 [56], P('uly'), may hold values from -1.5 to 1
- decay_rate: float32 [56], P('uly'), may hold values from 0.0003 to 0.05
- skip_gain: float32 [56], P('uly'), may hold values from 0.1 to 1.9
- state_in: bfloat16 [65536, 64], P('ctx'), may hold values from -0.75 to 0.75
- state_out: bfloat16 [65536, 64], P('ctx'), may hold values from -0.75 to 0.75
- segment_ids: int32 [65536], replicated, may hold values from 0 to 127, never falling along the last dimension, each value on 1 to 2048 neighbouring positions
Outputs:
- mixed: bfloat16 [65536, 3584], P(('ctx', 'uly'))
The draws below stay inside these ranges and needn't reach their ends.
Inputs may be any that keep to these rules, and one draw needn't show every extreme that they name: `segment_ids`: ids never fall along the sequence; every document holds at most 2048 tokens, and one holds exactly that many.
All inputs are finite; a program needn't handle non-finite values.
Results may differ from the reference program's by a relative error of at most 0.008.
Values may be sent and summed in bfloat16 or wider, within the bound.
No kernel may reach another device: no remote copies, remote signals or barrier semaphores. Data moves between devices by JAX's collectives and lax.ppermute only.
A program may use at most 128 MiB of HBM per device.

```python
import math
import jax
import jax.numpy as jnp
import numpy as np
from jax import lax

HEADS = 16
HEAD_DIM = 224
SSM_DIM = 64
STATE = 64
BLOCK = 256
REACH = 2
SSM_HEADS = 56
CTX_ROWS = 1024
SEQ = 65536
DOC_MOST = 2048
DOCS = 128
N_CTX = 64


def own_part(key):
    width = HEADS * HEAD_DIM
    return jnp.clip(jax.random.normal(key, (SEQ, width), jnp.float32), -6.0, 6.0)


def draw_queries(key, part):
    key = jax.random.fold_in(key, 11)
    own = own_part(key)
    return own.astype(jnp.bfloat16)


def draw_keys(key, part):
    key = jax.random.fold_in(key, 23)
    own = own_part(key)
    return own.astype(jnp.bfloat16)


def level_of(rng, shape, cuts, low, high):
    factor_of, own = 1.0, jax.random.fold_in(rng, 6)
    for axis_at, parts in cuts:
        heights = jnp.exp(jax.random.uniform(jax.random.fold_in(own, axis_at), (parts,), jnp.float32, low / len(cuts), high / len(cuts)))
        factor_of = factor_of * jnp.repeat(heights, shape[axis_at] // parts).reshape([-1 if axis == axis_at else 1 for axis in range(len(shape))])
    return factor_of


def split_up(amount, total, bound, slope):
    weights = [(1 << 20) // math.isqrt(rank ** slope) + 1 for rank in range(2, amount + 1)]
    spare, given = total - bound - (amount - 1), [1] * (amount - 1)
    while spare > 0:
        free = [i for i in range(amount - 1) if given[i] < bound]
        whole, budget = sum([weights[i] for i in free]), spare
        for i in free:
            extra = min(bound - given[i], max(1, budget * weights[i] // whole), spare)
            given[i] = given[i] + extra
            spare = spare - extra
    return np.array([bound] + given)


def uneven(rng, amount, total, limit, slope):
    if amount == 2:
        one = jax.random.randint(rng, (), max(1, total - limit), min(limit, total - 1) + 1)
        return jnp.stack([one, total - one])
    lengths = jnp.asarray(split_up(amount, total, limit, slope), jnp.int32)
    pairs = (amount - 1) // 2
    giver, sink = lengths[1:1 + 2 * pairs:2], lengths[2:2 + 2 * pairs:2]
    slack = jnp.minimum(giver - 1, limit - sink)
    passed = jax.random.randint(jax.random.fold_in(rng, 1), (pairs,), 0, 1 << 20) % (slack + 1)
    lengths = lengths.at[1:1 + 2 * pairs:2].set(giver - passed).at[2:2 + 2 * pairs:2].set(sink + passed)
    return lengths[jax.random.permutation(jax.random.fold_in(rng, 2), amount)]


def gaussian(rng, extent, scale, most, cuts=(), held_as=jnp.bfloat16):
    values = jax.random.normal(rng, extent, jnp.float32) * scale
    if len(cuts) > 0:
        values = level_of(rng, extent, cuts, -0.22, 0.18) * values
    return jnp.clip(values, min=-most, max=most).astype(held_as)


def setup_inputs(seed: int = 0) -> dict:
    splits = jax.random.split(jax.random.key(seed), 11)
    return {
        "queries": draw_queries(jax.random.fold_in(splits[10], 71), 0),
        "keys": draw_keys(jax.random.fold_in(splits[10], 71), 0),
        "values": gaussian(splits[2], (SEQ, HEADS * HEAD_DIM), 1.0, 6.0, ((0, 512),)),
        "step_raw": gaussian(splits[3], (SEQ, SSM_HEADS), 1.0, 4.0, ((0, 512),)),
        "step_bias": jnp.clip(-1.5 + 2.5 * jax.random.uniform(splits[4], (SSM_HEADS,), jnp.float32) ** level_of(splits[4], (SSM_HEADS,), ((0, 8),), -0.2, 0.2), -1.5, 1.0),
        "decay_rate": jnp.clip(jnp.exp(math.log(0.05) - 5.115996 * jax.random.uniform(splits[5], (SSM_HEADS,), jnp.float32) ** level_of(splits[5], (SSM_HEADS,), ((0, 8),), -0.2, 0.2)), 0.0003, 0.05),
        "skip_gain": jnp.clip(1.0 + 0.18 * jax.random.normal(splits[6], (SSM_HEADS,), jnp.float32), 0.1, 1.9),
        "state_in": gaussian(splits[7], (SEQ, STATE), STATE ** -0.5, 0.75, ((0, 64),)),
        "state_out": gaussian(splits[8], (SEQ, STATE), STATE ** -0.5, 0.75, ((0, 64),)),
        "segment_ids": jnp.searchsorted(jnp.cumsum(uneven(splits[9], DOCS, SEQ, DOC_MOST, 2)), jnp.arange(SEQ), side="right").astype(jnp.int32),
    }


def ssd_block(ssm_state, seg_before, x_blk, dt_blk, decay_rate, b_blk, c_blk, seg_blk):
    log_step = -dt_blk * decay_rate[None, :]
    running_log = jnp.cumsum(log_step, axis=0)
    blk_len = seg_blk.shape[0]
    offsets = jnp.arange(blk_len, dtype=jnp.int32)
    lower_mask = (offsets[:, None] >= offsets[None, :]) & (seg_blk[:, None] == seg_blk[None, :])
    by_head = jnp.transpose(running_log)
    log_gap = by_head[:, :, None] - by_head[:, None, :]
    decay_mat = jnp.where(lower_mask[None], jnp.exp(jnp.where(lower_mask[None], log_gap, 0.0)), 0.0)
    mixing = jnp.dot(c_blk, jnp.transpose(b_blk), preferred_element_type=jnp.float32)
    weighted = decay_mat * mixing[None] * jnp.transpose(dt_blk)[:, None, :]
    weighted = lax.optimization_barrier(weighted.astype(jnp.bfloat16)).astype(jnp.float32)
    y_local = jnp.einsum('hts,shp->thp', weighted, x_blk)
    c_wide = c_blk.astype(jnp.float32)
    b_wide = b_blk.astype(jnp.float32)
    enter_gain = jnp.exp(running_log) * (seg_blk == seg_before).astype(jnp.float32)[:, None]
    y_carried = jnp.einsum('tn,hnp->thp', c_wide, ssm_state, precision=lax.Precision.HIGHEST) * enter_gain[:, :, None]
    same_last = (seg_blk == seg_blk[-1]).astype(jnp.float32)[:, None]
    tail_gain = jnp.exp(running_log[-1][None, :] - running_log) * same_last * dt_blk
    keep_gain = jnp.exp(running_log[-1]) * (seg_blk[-1] == seg_before).astype(jnp.float32)
    new_state = jnp.einsum('sh,sn,shp->hnp', tail_gain, b_wide, x_blk, precision=lax.Precision.HIGHEST)
    new_state = new_state + ssm_state * keep_gain[:, None, None]
    return (new_state, y_local + y_carried)

def attend_window(q_blk, k_win, v_win, q_seg, k_seg, q_pos, k_pos):
    scores = jnp.einsum('rhe,whe->hrw', q_blk, k_win) / jnp.sqrt(jnp.float32(HEAD_DIM))
    allowed = (q_seg[:, None] == k_seg[None, :]) & (k_pos[None, :] <= q_pos[:, None])
    scores = jnp.where(allowed[None], scores, -1e+30)
    row_top = lax.optimization_barrier(jnp.max(scores, axis=2, keepdims=True))
    expo = jnp.exp(scores - row_top)
    row_total = lax.optimization_barrier(jnp.sum(expo, axis=2))
    weight = lax.optimization_barrier(expo.astype(jnp.bfloat16)).astype(jnp.float32)
    summed = jnp.einsum('hrw,whe->rhe', weight, v_win)
    return summed / jnp.transpose(row_total)[:, :, None]

def reference(queries, keys, values, step_raw, step_bias, decay_rate, skip_gain, state_in, state_out, segment_ids):
    width = HEADS * HEAD_DIM
    margin = REACH * CTX_ROWS
    q_all = queries.astype(jnp.float32).reshape(SEQ, HEADS, HEAD_DIM)
    k_pad = jnp.concatenate([jnp.zeros((margin, width), jnp.float32), keys.astype(jnp.float32)], axis=0)
    v_pad = jnp.concatenate([jnp.zeros((margin, width), jnp.float32), values.astype(jnp.float32)], axis=0)
    k_pad = k_pad.reshape(SEQ + margin, HEADS, HEAD_DIM)
    v_pad = v_pad.reshape(SEQ + margin, HEADS, HEAD_DIM)
    seg_pad = jnp.concatenate([jnp.full((margin,), -1, jnp.int32), segment_ids.astype(jnp.int32)])
    pos_pad = jnp.arange(SEQ + margin, dtype=jnp.int32) - margin

    def one_shard(shard):
        start = (shard * CTX_ROWS).astype(jnp.int32)
        q_blk = lax.dynamic_slice_in_dim(q_all, start, CTX_ROWS, 0)
        k_win = lax.dynamic_slice_in_dim(k_pad, start, margin + CTX_ROWS, 0)
        v_win = lax.dynamic_slice_in_dim(v_pad, start, margin + CTX_ROWS, 0)
        q_seg = lax.dynamic_slice_in_dim(segment_ids, start, CTX_ROWS, 0)
        k_seg = lax.dynamic_slice_in_dim(seg_pad, start, margin + CTX_ROWS, 0)
        q_pos = start + jnp.arange(CTX_ROWS, dtype=jnp.int32)
        k_pos = lax.dynamic_slice_in_dim(pos_pad, start, margin + CTX_ROWS, 0)
        result = attend_window(q_blk, k_win, v_win, q_seg, k_seg, q_pos, k_pos)
        return result.reshape(CTX_ROWS, width).astype(jnp.bfloat16)
    attended = lax.map(one_shard, jnp.arange(N_CTX, dtype=jnp.int32)).reshape(SEQ, width)
    x_all = attended.astype(jnp.float32).reshape(SEQ, SSM_HEADS, SSM_DIM)
    dt_all = jax.nn.softplus(step_raw.astype(jnp.float32) + step_bias[None, :])
    blk_len = min(BLOCK, CTX_ROWS)
    count = SEQ // blk_len
    inputs = (x_all.reshape(count, blk_len, SSM_HEADS, SSM_DIM), dt_all.reshape(count, blk_len, SSM_HEADS), state_in.reshape(count, blk_len, STATE), state_out.reshape(count, blk_len, STATE), segment_ids.reshape(count, blk_len))

    def advance(carried, pieces):
        ssm_state, seg_before = carried
        x_blk, dt_blk, b_blk, c_blk, seg_blk = pieces
        new_state, y_blk = ssd_block(ssm_state, seg_before, x_blk, dt_blk, decay_rate, b_blk, c_blk, seg_blk)
        return ((new_state, seg_blk[-1]), y_blk)
    start_state = (jnp.zeros((SSM_HEADS, STATE, SSM_DIM), jnp.float32), jnp.int32(-1))
    unused, outputs = lax.scan(advance, start_state, inputs)
    mixed = outputs.reshape(SEQ, SSM_HEADS, SSM_DIM) + skip_gain[None, :, None] * x_all
    return mixed.reshape(SEQ, width).astype(jnp.bfloat16)
```

```python
import functools
import math

import jax
import jax.numpy as jnp
from jax import lax
from jax.experimental import pallas as pl
from jax.experimental.pallas import tpu as pltpu
from jax.sharding import Mesh
from jax.sharding import PartitionSpec as P

HEADS = 16
HEAD_DIM = 224
SSM_DIM = 64
STATE = 64
ROWS = 128
PLANE = 4096
REACH = 2048
CHUNKS = 16
SSM = 4
WIDE = SSM * SSM_DIM
PACK = 464
LOG2E = math.log2(math.e)
NT = (((1,), (1,)), ((), ()))
VMEM_LIMIT = 56 * 1024 * 1024

f32, bf16, i32 = jnp.float32, jnp.bfloat16, jnp.int32


def iota(shape, dim):
    return lax.broadcasted_iota(i32, shape, dim)


def spread(rows, count=WIDE):
    width = rows.shape[-1]
    return jnp.concatenate(
        [jnp.broadcast_to(rows[r : r + 1, :], (SSM_DIM, width)) for r in range(SSM)], axis=0
    )


def pack_kernel(k_ref, v_ref, raw_ref, par_ref, out_ref):
    step = pl.program_id(0)
    kt = jnp.transpose(k_ref[...])
    vt = jnp.transpose(v_ref[...])
    rr, jj = iota((64, 56), 0), iota((64, 56), 1)
    head, r = 4 * step + (rr >> 4), rr & 15
    chosen = ((r < SSM) & (jj == ((7 * head) >> 1) + r)).astype(bf16)
    rows = lax.dot_general(chosen, raw_ref[...], NT, preferred_element_type=f32)
    whole = par_ref[...]
    high = whole.astype(bf16).astype(f32)
    mid = (whole - high).astype(bf16).astype(f32)
    low = whole - high - mid
    r = iota((64, ROWS), 0) & 15
    rows = jnp.where(r == 4, high, jnp.where(r == 5, mid, jnp.where(r == 6, low, rows))).astype(bf16)
    for h in range(4):
        out_ref[h, 0:224, :] = kt[224 * h : 224 * h + 224, :]
        out_ref[h, 224:448, :] = vt[224 * h : 224 * h + 224, :]
        out_ref[h, 448:464, :] = rows[16 * h : 16 * h + 16, :]


def pack(keys, values, step_raw, params):
    return pl.pallas_call(
        pack_kernel,
        grid=(4,),
        in_specs=[
            pl.BlockSpec((ROWS, 896), lambda i: (0, i)),
            pl.BlockSpec((ROWS, 896), lambda i: (0, i)),
            pl.BlockSpec((ROWS, 56), lambda i: (0, 0)),
            pl.BlockSpec((1, ROWS), lambda i: (0, 0)),
        ],
        out_specs=pl.BlockSpec((4, PACK, ROWS), lambda i: (i, 0, 0)),
        out_shape=jax.ShapeDtypeStruct((HEADS, PACK, ROWS), bf16),
        compiler_params=pltpu.CompilerParams(vmem_limit_bytes=VMEM_LIMIT),
        name="pack_keys_values",
    )(keys, values, step_raw, params)


def turn_kernel(own_ref, other_ref, out_ref):
    out_ref[0, 0:128, :] = jnp.transpose(own_ref[0])
    out_ref[0, 128:256, :] = jnp.transpose(other_ref[0])


def turn(own, other):
    count = own.shape[0]
    block = pl.BlockSpec((1, HEAD_DIM, ROWS), lambda i: (i, 0, 0))
    return pl.pallas_call(
        turn_kernel,
        grid=(count,),
        in_specs=[block, block],
        out_specs=pl.BlockSpec((1, 256, HEAD_DIM), lambda i: (i, 0, 0)),
        out_shape=jax.ShapeDtypeStruct((count, 256, HEAD_DIM), bf16),
        compiler_params=pltpu.CompilerParams(vmem_limit_bytes=VMEM_LIMIT),
        cost_estimate=pl.CostEstimate(flops=0, bytes_accessed=count * 256 * 256 * 4, transcendentals=0),
        name="turn_keys",
    )(own, other)


def prep_kernel(core_ref, par_ref, own_ref, other_ref, ds_ref, dso_ref, bc_ref, inner_ref, rows_ref, keep_ref):
    core = core_ref[0]
    shape = (CHUNKS * 16, ROWS)
    line, lane = iota(shape, 0), iota(shape, 1)
    r = line & 15
    bias, decay = jnp.zeros(shape, f32), jnp.zeros(shape, f32)
    for n in range(SSM):
        bias = jnp.where(r == n, par_ref[0, n], bias)
        decay = jnp.where(r == n, par_ref[1, n], decay)
    upper = (iota((ROWS, ROWS), 0) <= iota((ROWS, ROWS), 1)).astype(f32)

    def steps(ref, ids, which):
        raw = ref[...].reshape(shape).astype(f32)
        z = raw + bias
        dt = jnp.maximum(z, 0.0) + jnp.log1p(jnp.exp(-jnp.abs(z)))
        running = jnp.dot(-dt * decay, upper, precision=lax.Precision.HIGHEST, preferred_element_type=f32)
        start = 256 * (line >> 4) + 128 * which
        whole = jnp.broadcast_to(running[:, 127:128], shape)
        last = jnp.broadcast_to(ids[:, 127:128], shape)
        keep = jnp.where(last < start, jnp.exp(whole), 0.0)
        return dt, running, start, whole, last, keep

    ids = ds_ref[...].reshape(shape)
    dt, running, start, whole, last, keep = steps(own_ref, ids, core)
    tail = jnp.where(start + lane >= last, jnp.exp(whole - running) * dt, 0.0)
    enter = jnp.where(ids < start, jnp.exp(running), 0.0)
    keep_other = steps(other_ref, dso_ref[...].reshape(shape), 1 - core)[5]
    for b in range(CHUNKS):
        at = 16 * b
        rows_ref[b, 0:4, :] = tail[at : at + 4, :]
        rows_ref[b, 4:8, :] = enter[at : at + 4, :]
        keep_ref[b, 0:4, :] = jnp.where(core == 0, keep[at : at + 4, :], keep_other[at : at + 4, :])
        keep_ref[b, 4:8, :] = jnp.where(core == 0, keep_other[at : at + 4, :], keep[at : at + 4, :])
    running_t, dt_t = jnp.transpose(running), jnp.transpose(dt)
    s_at, t_at = iota((ROWS, ROWS), 0), iota((ROWS, ROWS), 1)
    for b in range(CHUNKS):
        at = 16 * b
        mix = lax.dot_general(
            bc_ref[b, :, 0:64], bc_ref[b, :, 64:128], NT, preferred_element_type=f32
        )
        base = 256 * b + 128 * core
        allowed = (s_at <= t_at) & (s_at >= ids[at : at + 1, :] - base)
        for n in range(SSM):
            gap = running[at + n : at + n + 1, :] - running_t[:, at + n : at + n + 1]
            value = jnp.exp(jnp.where(allowed, gap, 0.0)) * mix * dt_t[:, at + n : at + n + 1]
            inner_ref[b, n, :, :] = jnp.where(allowed, value, 0.0).astype(bf16)


def prep(core, params, own_steps, other_steps, ids, ids_other, bc):
    return pl.pallas_call(
        prep_kernel,
        in_specs=[pl.BlockSpec(memory_space=pltpu.SMEM)] * 2
        + [pl.BlockSpec(memory_space=pltpu.VMEM)] * 5,
        out_shape=(
            jax.ShapeDtypeStruct((CHUNKS, SSM, ROWS, ROWS), bf16),
            jax.ShapeDtypeStruct((CHUNKS, 8, ROWS), f32),
            jax.ShapeDtypeStruct((CHUNKS, 8, ROWS), f32),
        ),
        compiler_params=pltpu.CompilerParams(vmem_limit_bytes=VMEM_LIMIT),
        cost_estimate=pl.CostEstimate(flops=200_000_000, bytes_accessed=8_000_000, transcendentals=2_000_000),
        name="scan_weights",
    )(core, params, own_steps, other_steps, ids, ids_other, bc)


def attend_kernel(
    core_ref, low_ref, q_ref, kn_ref, knh_ref, own_ref, other_ref, hown_ref, hother_ref, ds_ref, rows_ref, bc_ref,
    keep_ref, x_ref, s_ref, send_ref, f_ref,
):
    core, off = core_ref[0], pl.multiple_of(core_ref[1], 32)
    scale = LOG2E / math.sqrt(HEAD_DIM)
    x_ref[...] = jnp.zeros_like(x_ref)
    line = iota((ROWS, 256), 0)
    lane = iota((1, 256), 1)

    def tile(i, carry):
        q = jnp.concatenate([q_ref[2 * i], q_ref[2 * i + 1]], axis=1)
        ids = jnp.concatenate([ds_ref[2 * i], ds_ref[2 * i + 1]], axis=1)
        q_at = 512 * i + 128 * core + (lane & 127) + 256 * (lane >> 7)

        def part(state, k_pair, v_parts, start, causal):
            top, total, acc = state
            pieces = []
            for j in range(4):
                at = start + 256 * (j // 2) + 128 * (core if j % 2 == 0 else 1 - core)
                k = k_pair[j // 2][128 * (j % 2) : 128 * (j % 2) + 128, :]
                score = jnp.dot(k, q, preferred_element_type=f32) * scale
                allowed = line >= ids - at
                if causal:
                    allowed = allowed & (line <= q_at - at)
                pieces.append(jnp.where(allowed, score, -1e30))
            score = jnp.concatenate(pieces, axis=0)
            new_top = jnp.maximum(top, jnp.max(score, axis=0, keepdims=True))
            expo = jnp.exp2(score - new_top)
            fade = jnp.exp2(top - new_top)
            total = total * fade + jnp.sum(expo, axis=0, keepdims=True)
            v = jnp.concatenate(v_parts, axis=1)
            acc = acc * fade + jnp.dot(v, expo.astype(bf16), preferred_element_type=f32)
            return new_top, total, acc

        def own(p, state, causal=False):
            k = (kn_ref[2 * p], kn_ref[2 * p + 1])
            v = [ref[2 * p + j, 224:448, :] for j in range(2) for ref in (own_ref, other_ref)]
            return part(state, k, v, 512 * p, causal)

        def halo(p, state):
            k = (knh_ref[2 * p], knh_ref[2 * p + 1])
            v = [ref[2 * p + j, 224:448, :] for j in range(2) for ref in (hown_ref, hother_ref)]
            return part(state, k, v, 512 * p - REACH, False)

        state = (
            jnp.full((1, 256), -1e30, f32),
            jnp.zeros((1, 256), f32),
            jnp.zeros((HEAD_DIM, 256), f32),
        )
        state = own(i, state, True)
        low = low_ref[i]
        state = lax.fori_loop(jnp.maximum(low, 0), i, own, state)
        state = lax.fori_loop(jnp.minimum(low + 4, 4), 4, halo, state)
        top, total, acc = state
        x = (acc / total).astype(bf16)
        x_ref[2 * i, pl.ds(off, HEAD_DIM), :] = x[:, 0:128]
        x_ref[2 * i + 1, pl.ds(off, HEAD_DIM), :] = x[:, 128:256]
        return carry

    lax.fori_loop(0, CHUNKS // 2, tile, 0)
    total = jnp.zeros((WIDE, STATE), f32)
    for b in range(CHUNKS):
        weighted = (x_ref[b].astype(f32) * spread(rows_ref[b, 0:4, :])).astype(bf16)
        state = jnp.dot(weighted, bc_ref[b, :, 0:64], preferred_element_type=f32)
        s_ref[b] = state
        send_ref[b % 8, :, 64 * (b // 8) : 64 * (b // 8) + 64] = state.astype(bf16)
        first = spread(keep_ref[b, 0:4, 0:64])
        second = spread(keep_ref[b, 4:8, 0:64])
        total = (first * second) * total + jnp.where(core == 0, second, 1.0) * state
    f_ref[...] = jnp.concatenate([total[0:128, :], total[128:256, :]], axis=1).astype(bf16)


def attend(core, low, q, kn, knh, own, other, hown, hother, ids, rows, bc, keep):
    return pl.pallas_call(
        attend_kernel,
        in_specs=[pl.BlockSpec(memory_space=pltpu.SMEM)] * 2
        + [pl.BlockSpec(memory_space=pltpu.VMEM)] * 11,
        out_shape=(
            jax.ShapeDtypeStruct((CHUNKS, WIDE, ROWS), bf16),
            jax.ShapeDtypeStruct((CHUNKS, WIDE, STATE), f32),
            jax.ShapeDtypeStruct((8, WIDE, 128), bf16),
            jax.ShapeDtypeStruct((128, 128), bf16),
        ),
        compiler_params=pltpu.CompilerParams(vmem_limit_bytes=VMEM_LIMIT),
        cost_estimate=pl.CostEstimate(flops=6_000_000_000, bytes_accessed=12_000_000, transcendentals=4_000_000),
        name="attend",
    )(core, low, q, kn, knh, own, other, hown, hother, ids, rows, bc, keep)


def local_kernel(par_ref, x_ref, inner_ref, y_ref):
    for b in range(CHUNKS):
        for n in range(SSM):
            x = x_ref[b, 64 * n : 64 * n + 64, :]
            y = jnp.dot(x, inner_ref[b, n], preferred_element_type=f32)
            y_ref[b, 64 * n : 64 * n + 64, :] = y + par_ref[2, n] * x.astype(f32)


def local(params, x, inner):
    return pl.pallas_call(
        local_kernel,
        in_specs=[pl.BlockSpec(memory_space=pltpu.SMEM)] + [pl.BlockSpec(memory_space=pltpu.VMEM)] * 2,
        out_shape=jax.ShapeDtypeStruct((CHUNKS, WIDE, ROWS), f32),
        compiler_params=pltpu.CompilerParams(vmem_limit_bytes=VMEM_LIMIT),
        cost_estimate=pl.CostEstimate(flops=150_000_000, bytes_accessed=6_000_000, transcendentals=0),
        name="scan_local",
    )(params, x, inner)


def carry_kernel(core_ref, y_ref, s_ref, other_ref, f_ref, g_ref, rows_ref, keep_ref, bc_ref, out_ref, hold):
    core, off = core_ref[0], pl.multiple_of(core_ref[1], 32)
    packed = f_ref[...].astype(f32) + g_ref[...].astype(f32)
    state = jnp.concatenate([packed[:, 0:64], packed[:, 64:128]], axis=0)
    for b in range(CHUNKS):
        mine = s_ref[b]
        theirs = other_ref[b % 8, :, 64 * (b // 8) : 64 * (b // 8) + 64].astype(f32)
        first, second = spread(keep_ref[b, 0:4, 0:64]), spread(keep_ref[b, 4:8, 0:64])
        middle = first * state + jnp.where(core == 0, mine, theirs)
        entering = jnp.where(core == 0, state, middle).astype(bf16)
        carried = lax.dot_general(entering, bc_ref[b, :, 64:128], NT, preferred_element_type=f32)
        hold[...] = y_ref[b] + carried * spread(rows_ref[b, 4:8, :])
        out_ref[b] = hold[pl.ds(off, HEAD_DIM), :].astype(bf16)
        state = second * middle + jnp.where(core == 0, theirs, mine)


def carry(core, y, s, other, f, g, rows, keep, bc):
    return pl.pallas_call(
        carry_kernel,
        in_specs=[pl.BlockSpec(memory_space=pltpu.SMEM)] + [pl.BlockSpec(memory_space=pltpu.VMEM)] * 8,
        out_shape=jax.ShapeDtypeStruct((CHUNKS, HEAD_DIM, ROWS), bf16),
        scratch_shapes=[pltpu.VMEM((WIDE, ROWS), f32)],
        compiler_params=pltpu.CompilerParams(vmem_limit_bytes=VMEM_LIMIT),
        name="scan_carry",
    )(core, y, s, other, f, g, rows, keep, bc)


def other_core(x):
    return lax.ppermute(x, "core", [(0, 1), (1, 0)])


def exchange(x):
    return lax.all_to_all(x, ("y", "x"), split_axis=0, concat_axis=0, tiled=True)


def document_starts(segment_ids, plane):
    padded = jnp.concatenate([jnp.full((REACH + 1,), -1, i32), segment_ids])
    window = lax.dynamic_slice_in_dim(padded, plane * PLANE, PLANE + REACH + 1, 0)
    place = jnp.arange(PLANE + REACH, dtype=i32) - REACH
    starts = jnp.where(window[1:] != window[:-1], place, -REACH).reshape(48, 128)
    within = lax.cummax(starts, axis=1)
    before = lax.cummax(within[:, 127], axis=0)
    before = jnp.concatenate([jnp.full((1,), -REACH, i32), before[:-1]])
    return jnp.maximum(within, before[:, None])[16:]


def on_device(
    queries, keys, values, step_raw, step_bias, decay_rate, skip_gain, state_in, state_out, segment_ids
):
    core, planes = lax.axis_index("core"), lax.axis_size("z")
    plane, head = lax.axis_index("z"), 4 * lax.axis_index("y") + lax.axis_index("x")

    both = jnp.concatenate([state_in, state_out], axis=1).reshape(4, 2, ROWS, 128)
    both = lax.dynamic_index_in_dim(both, core, 1, keepdims=False)
    bc = lax.all_gather(both, "y").reshape(CHUNKS, ROWS, 128)
    params = jnp.concatenate([step_bias, decay_rate, skip_gain, jnp.zeros((ROWS - 21,), f32)])[None]
    own = exchange(pack(keys, values, step_raw, params))
    other = other_core(own)
    following = [(i, i + 1) for i in range(planes - 1)]
    halo_own = lax.ppermute(own[8:, :448], "z", following)
    q = exchange(jnp.transpose(queries).reshape(HEADS, HEAD_DIM, ROWS))
    halo_other = other_core(halo_own)

    def whole(rows):
        return jnp.sum(rows[0:4, 452:455, 0:21].astype(f32), axis=1).reshape(4, 3, 7)

    mine, theirs = whole(own), whole(other)
    zero = jnp.where(core == 0, mine, theirs)
    one = jnp.where(core == 0, theirs, mine)
    table = jnp.stack([zero, one], axis=1).transpose(2, 0, 1, 3).reshape(3, 56)
    mamba = lax.dynamic_slice_in_dim(table, (7 * head) >> 1, SSM, 1)

    starts = document_starts(segment_ids, plane).reshape(CHUNKS, 2, ROWS)
    ids = lax.dynamic_index_in_dim(starts, core, 1, keepdims=False)
    ids_other = lax.dynamic_index_in_dim(starts, 1 - core, 1, keepdims=False)
    low = ids[0::2, 0] >> 9
    where = jnp.stack([core, 32 * (head & 1)]).astype(i32)

    def wide(x):
        return jnp.broadcast_to(x[:, None, :], (CHUNKS, 16, ROWS))

    inner, rows, keep = prep(
        where, mamba, own[:, 448:464], other[:, 448:464], wide(ids), wide(ids_other), bc
    )
    kn = turn(own, other)
    knh = turn(halo_own, halo_other)
    x, s, send, final = attend(
        where, low, q, kn, knh, own, other, halo_own, halo_other, ids[:, None, :], rows, bc, keep
    )
    s_other = other_core(send)
    same = lax.ppermute(final, "z", following)
    cross = lax.ppermute(
        final, ("z", "core"), [(2 * i + c, 2 * i + 3 - c) for i in range(planes - 1) for c in range(2)]
    )
    y = local(mamba, x, inner)
    mixed = exchange(carry(where, y, s, s_other, same, cross, rows, keep, bc))
    return jnp.transpose(mixed.reshape(HEADS * HEAD_DIM, ROWS))


def solution(mesh):
    devices = mesh.devices.reshape(-1, 4, 4, 2)
    return jax.shard_map(
        on_device,
        mesh=Mesh(devices, ("z", "y", "x", "core")),
        in_specs=(
            P(("z", "y", "x", "core"), None),
            P(("z", "y", "x", "core"), None),
            P(("z", "y", "x", "core"), None),
            P(("z", "y", "x", "core"), None),
            P(("x", "core")),
            P(("x", "core")),
            P(("x", "core")),
            P(("z", "y"), None),
            P(("z", "y"), None),
            P(),
        ),
        out_specs=P(("z", "y", "x", "core"), None),
        check_vma=False,
    )
```

```python
import functools
import math

import jax
import jax.numpy as jnp
from jax import lax
from jax.experimental import pallas as pl
from jax.experimental.pallas import tpu as pltpu
from jax.sharding import Mesh
from jax.sharding import PartitionSpec as P

HEADS = 16
HEAD_DIM = 224
SSM_DIM = 64
STATE = 64
ROWS = 128
PLANE = 4096
REACH = 2048
CHUNKS = 16
SSM = 4
WIDE = SSM * SSM_DIM
KV = 480
FIRST = 496
LOG2E = math.log2(math.e)
NT = (((1,), (1,)), ((), ()))
VMEM_LIMIT = 20 * 1024 * 1024

f32, bf16, i32 = jnp.float32, jnp.bfloat16, jnp.int32


def in_hbm(x):
    return pltpu.with_memory_space_constraint(x, pltpu.HBM)


def iota(shape, dim):
    return lax.broadcasted_iota(i32, shape, dim)


def spread(rows):
    width = rows.shape[-1]
    return jnp.concatenate(
        [jnp.broadcast_to(rows[r : r + 1, :], (SSM_DIM, width)) for r in range(SSM)], axis=0
    )


def parts(x):
    high = x.astype(bf16).astype(f32)
    mid = (x - high).astype(bf16).astype(f32)
    return high, mid, x - high - mid


def pack_first_kernel(bias_ref, decay_ref, skip_ref, k_ref, v_ref, raw_ref, out_ref):
    step = pl.program_id(0)
    vt = jnp.transpose(v_ref[...])
    rr, jj = iota((64, 56), 0), iota((64, 56), 1)
    head, r = 4 * step + (rr >> 4), rr & 15
    chosen = ((r < SSM) & (jj == ((7 * head) >> 1) + r)).astype(bf16)
    rows = jnp.dot(chosen, raw_ref[...], preferred_element_type=f32)
    lane = iota((1, ROWS), 1)
    whole = jnp.zeros((1, ROWS), f32)
    for n, ref in enumerate((bias_ref, decay_ref, skip_ref)):
        for j in range(7):
            whole = jnp.where(lane == 7 * n + j, ref[j], whole)
    high, mid, low = parts(whole)
    r = iota((64, ROWS), 0) & 15
    rows = jnp.where(r == 4, high, jnp.where(r == 5, mid, jnp.where(r == 6, low, rows))).astype(bf16)
    for h in range(4):
        k = k_ref[:, 224 * h : 224 * h + 224]
        out_ref[h, 0:128, :] = k[:, 0:128]
        out_ref[h, 128:256, :] = jnp.concatenate([k[:, 128:224], jnp.zeros((ROWS, 32), bf16)], axis=1)
        out_ref[h, 256:480, :] = vt[224 * h : 224 * h + 224, :]
        out_ref[h, 480:496, :] = rows[16 * h : 16 * h + 16, :]


def pack_first(keys, values, raw, step_bias, decay_rate, skip_gain):
    return pl.pallas_call(
        pack_first_kernel,
        grid=(4,),
        in_specs=[pl.BlockSpec(memory_space=pltpu.SMEM)] * 3
        + [pl.BlockSpec((ROWS, 896), lambda i: (0, i))] * 2
        + [pl.BlockSpec((56, ROWS), lambda i: (0, 0))],
        out_specs=pl.BlockSpec((4, FIRST, ROWS), lambda i: (i, 0, 0)),
        out_shape=jax.ShapeDtypeStruct((HEADS, FIRST, ROWS), bf16),
        name="pack_keys_values",
    )(step_bias, decay_rate, skip_gain, keys, values, raw)


VMEM = pl.BlockSpec(memory_space=pltpu.VMEM)
ANYWHERE = pl.BlockSpec(memory_space=pl.ANY)
SMEM = pl.BlockSpec(memory_space=pltpu.SMEM)
HBM = pl.BlockSpec(memory_space=pltpu.HBM)
CORE, OFFSET, Y_AT, FIRST_MAMBA, LOW = range(5)
NUMBERS = LOW + 4


def cut_kernel(first_ref, before_ref, out_ref):
    out_ref[...] = first_ref[8:16, 0:KV, :]


def cut(first, before):
    return pl.pallas_call(
        cut_kernel,
        in_specs=[VMEM, ANYWHERE],
        out_specs=VMEM,
        out_shape=jax.ShapeDtypeStruct((8, KV, ROWS), bf16),
        compiler_params=pltpu.CompilerParams(vmem_limit_bytes=VMEM_LIMIT),
        name="cut_halo",
    )(first, before)


def gate_kernel(*refs):
    pass


def gate(x, *before):
    return pl.pallas_call(
        gate_kernel,
        in_specs=[HBM] + [ANYWHERE] * len(before),
        out_specs=HBM,
        out_shape=pltpu.HBM(x.shape, x.dtype),
        input_output_aliases={0: 0},
        name="gate",
    )(in_hbm(x), *before)


def tie_kernel(first_ref, *refs):
    refs[-2][...] = first_ref[...]


def tie(first, q, *before):
    return pl.pallas_call(
        tie_kernel,
        in_specs=[VMEM] + [ANYWHERE] * (1 + len(before)),
        out_specs=(VMEM, ANYWHERE),
        out_shape=(jax.ShapeDtypeStruct(first.shape, first.dtype), jax.ShapeDtypeStruct(q.shape, q.dtype)),
        input_output_aliases={0: 0, 1: 1},
        compiler_params=pltpu.CompilerParams(vmem_limit_bytes=VMEM_LIMIT),
        name="tie",
    )(first, q, *before)


def step_sizes(raw, bias, decay):
    z = raw + bias
    dt = jnp.maximum(z, 0.0) + jnp.log1p(jnp.exp(-jnp.abs(z)))
    return dt, -dt * decay


def prep_kernel(
    num_ref, own_ref, other_ref, ds_ref, b0_ref, b1_ref, b2_ref, b3_ref, inner_ref, rows_ref, par_ref, bc_ref, sems
):
    core = num_ref[CORE]
    copies = [
        pltpu.make_async_copy(ref, bc_ref.at[pl.ds(4 * ((num_ref[Y_AT] - d) & 3), 4)], sems.at[d])
        for d, ref in enumerate((b0_ref, b1_ref, b2_ref, b3_ref))
    ]
    for copy in copies:
        copy.start()
    shape = (CHUNKS * 16, ROWS)
    line, lane = iota(shape, 0), iota(shape, 1)
    r = line & 15
    bias, decay = jnp.zeros(shape, f32), jnp.zeros(shape, f32)
    par_ref[...] = jnp.zeros_like(par_ref)
    for n in range(SSM):
        mamba = num_ref[FIRST_MAMBA] + n
        holder = (mamba * 37) >> 8
        at = mamba - 7 * holder
        held = jnp.where((holder & 1) == core, own_ref[holder >> 1], other_ref[holder >> 1]).astype(f32)
        held = held[4:5, :] + held[5:6, :] + held[6:7, :]

        def value(which):
            chosen = jnp.where(iota((1, ROWS), 1) == 7 * which + at, held, 0.0)
            return jnp.sum(chosen, axis=1, keepdims=True)

        for which in range(3):
            par_ref[4 * which + n : 4 * which + n + 1, :] = jnp.broadcast_to(value(which), (1, ROWS))
        bias = jnp.where(r == n, value(0), bias)
        decay = jnp.where(r == n, value(1), decay)
    upper = (iota((ROWS, ROWS), 0) <= iota((ROWS, ROWS), 1)).astype(f32)
    ids = spread_ids(ds_ref, 0)
    dt, log_step = step_sizes(own_ref[...].reshape(shape).astype(f32), bias, decay)
    running = jnp.dot(log_step, upper, precision=lax.Precision.HIGHEST, preferred_element_type=f32)
    start = 256 * (line >> 4) + 128 * core
    whole = jnp.broadcast_to(running[:, 127:128], shape)
    last = jnp.broadcast_to(ids[:, 127:128], shape)
    tail = jnp.where(start + lane >= last, jnp.exp(whole - running) * dt, 0.0)
    enter = jnp.where(ids < start, jnp.exp(running), 0.0)
    for b in range(CHUNKS):
        at = 16 * b
        rows_ref[b, 0:4, :] = tail[at : at + 4, :]
        rows_ref[b, 4:8, :] = enter[at : at + 4, :]
    running_t, dt_t = jnp.transpose(running), jnp.transpose(dt)
    s_at, t_at = iota((ROWS, ROWS), 0), iota((ROWS, ROWS), 1)
    for copy in copies:
        copy.wait()
    for b in range(CHUNKS):
        at = 16 * b
        state_in = jnp.transpose(bc_ref[b, 0:64, :].astype(f32)).astype(bf16)
        mix = jnp.dot(state_in, bc_ref[b, 64:128, :], preferred_element_type=f32)
        base = 256 * b + 128 * core
        allowed = (s_at <= t_at) & (s_at >= ids[at : at + 1, :] - base)
        for n in range(SSM):
            gap = running[at + n : at + n + 1, :] - running_t[:, at + n : at + n + 1]
            value = jnp.exp(jnp.where(allowed, gap, 0.0)) * mix * dt_t[:, at + n : at + n + 1]
            inner_ref[b, n, :, :] = jnp.where(allowed, value, 0.0).astype(bf16)


def spread_ids(ds_ref, which):
    return jnp.concatenate(
        [jnp.broadcast_to(ds_ref[b, which : which + 1, :], (16, ROWS)) for b in range(CHUNKS)], axis=0
    )


STEPS = pl.BlockSpec((CHUNKS, 16, ROWS), lambda i: (0, 30, 0))


def prep(numbers, own, other, ids, maps):
    return pl.pallas_call(
        prep_kernel,
        grid=(1,),
        in_specs=[SMEM, STEPS, STEPS, VMEM] + [ANYWHERE] * 4,
        out_shape=(
            jax.ShapeDtypeStruct((CHUNKS, SSM, ROWS, ROWS), bf16),
            jax.ShapeDtypeStruct((CHUNKS, 8, ROWS), f32),
            jax.ShapeDtypeStruct((16, ROWS), f32),
            jax.ShapeDtypeStruct((CHUNKS, 128, ROWS), bf16),
        ),
        out_specs=(VMEM,) * 4,
        scratch_shapes=[pltpu.SemaphoreType.DMA((4,))],
        compiler_params=pltpu.CompilerParams(vmem_limit_bytes=VMEM_LIMIT),
        cost_estimate=pl.CostEstimate(flops=200_000_000, bytes_accessed=8_000_000, transcendentals=2_000_000),
        name="scan_weights",
    )(numbers, own, other, ids, *maps)


def keep_kernel(num_ref, par_ref, own_ref, other_ref, ds_ref, keep_ref):
    core = num_ref[CORE]
    shape = (CHUNKS * 16, ROWS)
    line = iota(shape, 0)
    bias = jnp.concatenate([par_ref[0:4, :], jnp.zeros((12, ROWS), f32)] * CHUNKS, axis=0)
    decay = jnp.concatenate([par_ref[4:8, :], jnp.zeros((12, ROWS), f32)] * CHUNKS, axis=0)

    def keep(which):
        at = jnp.where(which == core, 0, 1)
        ids = jnp.where(at == 0, spread_ids(ds_ref, 0), spread_ids(ds_ref, 1))
        raw = jnp.where(at == 0, own_ref[...], other_ref[...]).reshape(shape).astype(f32)
        whole = jnp.sum(step_sizes(raw, bias, decay)[1], axis=1, keepdims=True)
        value = jnp.where(ids[:, 127:128] < 256 * (line[:, 0:1] >> 4) + 128 * which, jnp.exp(whole), 0.0)
        return jnp.broadcast_to(value, shape)

    for which in range(2):
        kept = keep(which)
        for b in range(CHUNKS):
            keep_ref[b, 4 * which : 4 * which + 4, :] = kept[16 * b : 16 * b + 4, :]


def keeps(numbers, params, own, other, ids):
    return pl.pallas_call(
        keep_kernel,
        grid=(1,),
        in_specs=[SMEM, VMEM, STEPS, STEPS, VMEM],
        out_specs=VMEM,
        out_shape=jax.ShapeDtypeStruct((CHUNKS, 8, ROWS), f32),
        compiler_params=pltpu.CompilerParams(vmem_limit_bytes=VMEM_LIMIT),
        name="scan_keeps",
    )(numbers, params, own, other, ids)


class Tiles:
    def __init__(self, core, shift, own, other, q, ds, scratch):
        self.core, self.shift, self.refs, self.q, self.ds = core, shift, (own, other), q, ds
        self.even, self.odd, self.turned = scratch

    def start(self, tile):
        for n in range(4):
            self.turned[0:HEAD_DIM, 128 * n : 128 * n + 128] = self.q[4 * tile + n]
        self.turned[HEAD_DIM:256, :] = jnp.zeros((32, 512), bf16)
        self.ids = jnp.concatenate([self.ds[4 * tile + n, 0:1, :] for n in range(4)], axis=1)
        lane = iota((1, 512), 1)
        self.q_at = 1024 * tile + 128 * self.core + (lane & 127) + 256 * (lane >> 7)

    def score(self, p, s, lanes=slice(0, 512)):
        k = jnp.concatenate(
            [
                jnp.concatenate([ref[2 * p + j, 0:128, :], ref[2 * p + j, 128:256, :]], axis=1)
                for j in range(2)
                for ref in self.refs
            ],
            axis=0,
        )
        s[:, lanes] = jnp.dot(k, self.turned[:, lanes], preferred_element_type=f32)

    def absorb(self, p, s, acc_ref, stat_ref, lanes=slice(0, 512), causal=False, valid=True):
        width = lanes.stop - lanes.start
        scale = LOG2E / math.sqrt(HEAD_DIM)
        line = iota((ROWS, width), 0)
        ids = jnp.where(valid, self.ids[:, lanes], 1 << 20)
        pieces = []
        for j in range(4):
            at = 512 * p + self.shift + 256 * (j // 2) + 128 * (self.core if j % 2 == 0 else 1 - self.core)
            allowed = line >= ids - at
            if causal:
                allowed = allowed & (line <= self.q_at[:, lanes] - at)
            pieces.append(jnp.where(allowed, s[128 * j : 128 * j + 128, lanes], -1e30))
        masked = jnp.concatenate(pieces, axis=0)
        top = stat_ref[0:1, lanes]
        new_top = jnp.maximum(top, jnp.max(masked, axis=0, keepdims=True))
        expo = jnp.exp2((masked - new_top) * scale)
        fade = jnp.exp2((top - new_top) * scale)
        stat_ref[1:2, lanes] = stat_ref[1:2, lanes] * fade + jnp.sum(expo, axis=0, keepdims=True)
        stat_ref[0:1, lanes] = new_top
        v = jnp.concatenate([ref[2 * p + j, 256:480, :] for j in range(2) for ref in self.refs], axis=1)
        acc_ref[:, lanes] = acc_ref[:, lanes] * fade + jnp.dot(v, expo.astype(bf16), preferred_element_type=f32)

    def back(self, p, low, acc_ref, stat_ref):
        def two(n, carry):
            at = p - 2 * n
            self.score(jnp.maximum(at - 1, 0), self.odd)
            self.absorb(at, self.even, acc_ref, stat_ref)
            self.score(jnp.maximum(at - 2, 0), self.even)
            self.absorb(jnp.maximum(at - 1, 0), self.odd, acc_ref, stat_ref, valid=at - 1 >= low)
            return carry

        lax.fori_loop(0, jnp.maximum(p - low + 2, 0) >> 1, two, 0)


def buffers(tiles):
    return [
        pltpu.VMEM((512, 512), f32),
        pltpu.VMEM((512, 512), f32),
        pltpu.VMEM((256, 512), bf16),
        pltpu.VMEM((tiles, HEAD_DIM, 512), f32),
        pltpu.VMEM((tiles, 8, 512), f32),
    ]


def own_states(x_ref, rows_ref, keep_ref, maps_ref, send_ref, core):
    total = jnp.zeros((WIDE, STATE), f32)
    for pair in range(4):
        states = []
        for b in (2 * pair, 2 * pair + 1):
            weighted = (x_ref[b].astype(f32) * spread(rows_ref[b, 0:4, :])).astype(bf16)
            state = lax.dot_general(weighted, maps_ref[b, 0:64, :], NT, preferred_element_type=f32)
            states.append(state)
            first, second = spread(keep_ref[b, 0:4, 0:64]), spread(keep_ref[b, 4:8, 0:64])
            total = (first * second) * total + jnp.where(core == 0, second, 1.0) * state
        send_ref[pair] = jnp.concatenate(states, axis=1).astype(bf16)
    return total


def start_all(copies):
    for copy in copies:
        copy.start()


def wait_all(copies):
    for copy in copies:
        copy.wait()


def put_x(x_ref, at, off, acc, total):
    x = (acc / total).astype(bf16)
    for n in range(4):
        x_ref[at + n, pl.ds(off, HEAD_DIM), :] = x[:, 128 * n : 128 * n + 128]


def near_kernel(
    num_any, q_ref, own_ref, other_ref, ds_ref, rows_any, keep_any, maps_any,
    x_out, send_out, left_ref, acc_out, stat_out,
    even, odd, turned, acc_ref, stat_ref, rows_ref, keep_ref, maps_ref, x_ref, send_ref, num_ref, sems,
):
    numbers = pltpu.make_async_copy(num_any, num_ref, sems.at[7])
    numbers.start()
    reads = [
        pltpu.make_async_copy(ref.at[pl.ds(8, 8)], to, sems.at[n])
        for n, (ref, to) in enumerate(((rows_any, rows_ref), (keep_any, keep_ref), (maps_any, maps_ref)))
    ]
    start_all(reads)
    x_ref[...] = jnp.zeros_like(x_ref)
    acc_ref[...] = jnp.zeros_like(acc_ref)
    stat_ref[...] = jnp.where(iota(stat_ref.shape, 1) == 0, -1e30, 0.0)
    numbers.wait()
    core, off = num_ref[CORE], pl.multiple_of(num_ref[OFFSET], 32)
    tiles = Tiles(core, 0, own_ref, other_ref, q_ref, ds_ref, (even, odd, turned))
    late = slice(256, 512)
    for i in range(4):
        acc, stat = acc_ref.at[i], stat_ref.at[i]
        tiles.start(i)
        tiles.score(2 * i + 1, odd, late)
        tiles.score(2 * i, even)
        tiles.absorb(2 * i + 1, odd, acc, stat, late, causal=True)
        tiles.score(max(2 * i - 1, 0), odd)
        tiles.absorb(2 * i, even, acc, stat, causal=True)
        tiles.even, tiles.odd = odd, even
        tiles.back(2 * i - 1, jnp.maximum(num_ref[LOW + i], 0), acc, stat)
        tiles.even, tiles.odd = even, odd
    writes = [
        pltpu.make_async_copy(acc_ref.at[pl.ds(0, 2)], acc_out, sems.at[3]),
        pltpu.make_async_copy(stat_ref.at[pl.ds(0, 2)], stat_out, sems.at[4]),
        pltpu.make_async_copy(x_ref, x_out, sems.at[5]),
        pltpu.make_async_copy(send_ref, send_out, sems.at[6]),
    ]
    start_all(writes[0:2])
    for i in range(2, 4):
        put_x(x_ref, 4 * i - 8, off, acc_ref[i], stat_ref[i, 1:2, :])
    start_all(writes[2:3])
    wait_all(reads)
    total = own_states(x_ref, rows_ref, keep_ref, maps_ref, send_ref, core)
    start_all(writes[3:4])
    left_ref[...] = jnp.concatenate([total[0:128, :], total[128:256, :]], axis=1).astype(bf16)
    wait_all(writes)


STATE_BUFFERS = [
    pltpu.VMEM((8, 8, ROWS), f32),
    pltpu.VMEM((8, 8, ROWS), f32),
    pltpu.VMEM((8, 128, ROWS), bf16),
]


def attend_near(numbers, q, own, other, ids, rows, keep, maps):
    return pl.pallas_call(
        near_kernel,
        in_specs=[HBM] + [VMEM] * 4 + [HBM] * 3,
        out_specs=(HBM, HBM, VMEM, HBM, HBM),
        out_shape=(
            pltpu.HBM((8, WIDE, ROWS), bf16),
            pltpu.HBM((4, WIDE, 128), bf16),
            jax.ShapeDtypeStruct((128, 128), bf16),
            pltpu.HBM((2, HEAD_DIM, 512), f32),
            pltpu.HBM((2, 8, 512), f32),
        ),
        scratch_shapes=buffers(4)
        + STATE_BUFFERS
        + [
            pltpu.VMEM((8, WIDE, ROWS), bf16),
            pltpu.VMEM((4, WIDE, 128), bf16),
            pltpu.SMEM((NUMBERS,), i32),
            pltpu.SemaphoreType.DMA((8,)),
        ],
        compiler_params=pltpu.CompilerParams(vmem_limit_bytes=VMEM_LIMIT),
        cost_estimate=pl.CostEstimate(flops=5_000_000_000, bytes_accessed=9_000_000, transcendentals=4_000_000),
        name="attend_near",
    )(in_hbm(numbers), q, own, other, ids, in_hbm(rows), in_hbm(keep), in_hbm(maps))


def far_kernel(
    num_any, q_ref, own_any, other_ref, ds_ref, came_ref, acc_any, stat_any, rows_any, keep_any, maps_any, late_any,
    x_ref, send_ref, even, odd, turned, acc_ref, stat_ref, rows_ref, keep_ref, maps_ref, own_ref, num_ref, sems,
):
    reads = [
        pltpu.make_async_copy(num_any, num_ref, sems.at[0]),
        pltpu.make_async_copy(own_any, own_ref, sems.at[1]),
        pltpu.make_async_copy(acc_any, acc_ref, sems.at[2]),
        pltpu.make_async_copy(stat_any, stat_ref, sems.at[3]),
        pltpu.make_async_copy(late_any, send_ref.at[pl.ds(4, 4)], sems.at[4]),
        pltpu.make_async_copy(rows_any.at[pl.ds(0, 8)], rows_ref, sems.at[5]),
        pltpu.make_async_copy(keep_any.at[pl.ds(0, 8)], keep_ref, sems.at[6]),
        pltpu.make_async_copy(maps_any.at[pl.ds(0, 8)], maps_ref, sems.at[7]),
    ]
    start_all(reads)
    x_ref[...] = jnp.zeros_like(x_ref)
    send_ref[8, 0:128, :] = came_ref[...]
    send_ref[8, 128:256, :] = jnp.zeros((128, 128), bf16)
    wait_all(reads[0:4])
    core, off = num_ref[CORE], pl.multiple_of(num_ref[OFFSET], 32)
    tiles = Tiles(core, -REACH, own_ref, other_ref, q_ref, ds_ref, (even, odd, turned))
    for i in range(2):
        low = jnp.clip(num_ref[LOW + i] + 4, 0, 4)

        @pl.when(low < 4)
        def _():
            tiles.start(i)
            tiles.score(3, even)
            tiles.back(3, low, acc_ref.at[i], stat_ref.at[i])

        put_x(x_ref, 4 * i, off, acc_ref[i], stat_ref[i, 1:2, :])
    wait_all(reads[4:])
    own_states(x_ref, rows_ref, keep_ref, maps_ref, send_ref, core)


def attend_far(numbers, q, own, other, ids, came, acc, stat, rows, keep, maps, late_states):
    return pl.pallas_call(
        far_kernel,
        in_specs=[HBM, VMEM, HBM] + [VMEM] * 3 + [HBM] * 6,
        out_specs=(VMEM,) * 2,
        out_shape=(
            jax.ShapeDtypeStruct((8, WIDE, ROWS), bf16),
            jax.ShapeDtypeStruct((9, WIDE, 128), bf16),
        ),
        scratch_shapes=buffers(2)
        + STATE_BUFFERS
        + [
            pltpu.VMEM((8, KV, ROWS), bf16),
            pltpu.SMEM((NUMBERS,), i32),
            pltpu.SemaphoreType.DMA((8,)),
        ],
        compiler_params=pltpu.CompilerParams(vmem_limit_bytes=VMEM_LIMIT),
        cost_estimate=pl.CostEstimate(flops=2_000_000_000, bytes_accessed=5_000_000, transcendentals=1_000_000),
        name="attend_far",
    )(
        in_hbm(numbers), q, in_hbm(own), other, ids, came, in_hbm(acc), in_hbm(stat), in_hbm(rows), in_hbm(keep),
        in_hbm(maps), in_hbm(late_states),
    )


def scan_kernel(
    num_ref, par_ref, xe_ref, xl_ref, inner_ref, own_ref, other_ref, f_ref, g_ref, rows_ref, keep_ref, bc_ref,
    out_ref, state_ref, hold,
):
    step = pl.program_id(0)
    core, off = num_ref[CORE], pl.multiple_of(num_ref[OFFSET], 32)
    early = step < 2

    @pl.when(step == 0)
    def _():
        packed = f_ref[0, 0:128, :].astype(f32) + g_ref[0, 0:128, :].astype(f32)
        state_ref[0:128, :] = packed[:, 0:64]
        state_ref[128:256, :] = packed[:, 64:128]

    state = state_ref[...]
    for b in range(4):
        at = slice(64 * (b % 2), 64 * (b % 2) + 64)
        mine, theirs = own_ref[b // 2, :, at].astype(f32), other_ref[b // 2, :, at].astype(f32)
        first, second = spread(keep_ref[b, 0:4, 0:64]), spread(keep_ref[b, 4:8, 0:64])
        middle = first * state + jnp.where(core == 0, mine, theirs)
        entering = jnp.where(core == 0, state, middle).astype(bf16)
        state = second * middle + jnp.where(core == 0, theirs, mine)
        carried = jnp.dot(entering, bc_ref[b, 64:128, :], preferred_element_type=f32)
        enter = rows_ref[b, 4:8, :]
        for n in range(SSM):
            rows = slice(64 * n, 64 * n + 64)
            x = jnp.where(early, xe_ref[b, rows, :], xl_ref[b, rows, :])
            y = jnp.dot(x, inner_ref[b, n], preferred_element_type=f32)
            hold[b, rows, :] = y + par_ref[8 + n : 9 + n, :] * x.astype(f32) + carried[rows] * enter[n : n + 1, :]
        out_ref[b] = hold[b, pl.ds(off, HEAD_DIM), :].astype(bf16)
    state_ref[...] = state


def scan(numbers, params, x, inner, own, other, rows, keep, maps):
    def chunks(*shape):
        return pl.BlockSpec(shape, lambda i: (i,) + (0,) * (len(shape) - 1))

    def halves(*shape):
        zeros = (0,) * (len(shape) - 1)
        return [
            pl.BlockSpec(shape, lambda i: (jnp.minimum(i, 1),) + zeros),
            pl.BlockSpec(shape, lambda i: (jnp.maximum(i - 2, 0),) + zeros),
        ]

    return pl.pallas_call(
        scan_kernel,
        grid=(4,),
        in_specs=[SMEM, pl.BlockSpec((16, ROWS), lambda i: (0, 0))]
        + halves(4, WIDE, ROWS)
        + [chunks(4, SSM, ROWS, ROWS)]
        + [chunks(2, WIDE, 128)] * 2
        + [pl.BlockSpec((1, WIDE, 128), lambda i: (8, 0, 0))] * 2
        + [chunks(4, 8, ROWS), chunks(4, 8, ROWS), chunks(4, 128, ROWS)],
        out_specs=chunks(4, HEAD_DIM, ROWS),
        out_shape=jax.ShapeDtypeStruct((CHUNKS, HEAD_DIM, ROWS), bf16),
        scratch_shapes=[pltpu.VMEM((WIDE, STATE), f32), pltpu.VMEM((4, WIDE, ROWS), f32)],
        compiler_params=pltpu.CompilerParams(vmem_limit_bytes=VMEM_LIMIT),
        name="scan",
    )(numbers, params, *x, inner, own, other, own, other, rows, keep, maps)


def other_core(x):
    return lax.ppermute(x, "core", [(0, 1), (1, 0)])


def exchange(x):
    return lax.all_to_all(x, ("y", "x"), split_axis=0, concat_axis=0, tiled=True)


def document_starts(segment_ids, plane):
    padded = jnp.concatenate([jnp.full((REACH + 1,), -1, i32), segment_ids])
    window = lax.dynamic_slice_in_dim(padded, plane * PLANE, PLANE + REACH + 1, 0)
    place = jnp.arange(PLANE + REACH, dtype=i32) - REACH
    starts = jnp.where(window[1:] != window[:-1], place, -REACH).reshape(48, 128)
    within = lax.cummax(starts, axis=1)
    before = lax.cummax(within[:, 127], axis=0)
    before = jnp.concatenate([jnp.full((1,), -REACH, i32), before[:-1]])
    return jnp.maximum(within, before[:, None])[16:]


def on_device(
    queries, keys, values, step_raw, step_bias, decay_rate, skip_gain, state_in, state_out, segment_ids
):
    core, planes = lax.axis_index("core"), lax.axis_size("z")
    plane, head = lax.axis_index("z"), 4 * lax.axis_index("y") + lax.axis_index("x")
    following = [(i, i + 1) for i in range(planes - 1)]

    first = exchange(pack_first(keys, values, jnp.transpose(step_raw), step_bias, decay_rate, skip_gain))
    both = jnp.concatenate([jnp.transpose(state_in), jnp.transpose(state_out)], axis=0).reshape(128, 4, 2, ROWS)
    both = jnp.transpose(lax.dynamic_index_in_dim(both, core, 2, keepdims=False), (1, 0, 2))
    maps = [both] + [lax.ppermute(both, "y", [(i, (i + d) % 4) for i in range(4)]) for d in range(1, 4)]

    starts = document_starts(segment_ids, plane).reshape(CHUNKS, 2, ROWS)
    ids = jnp.where(core == 0, starts, starts[:, ::-1])
    low = ids[0::4, 0, 0] >> 9
    numbers = [core, 32 * (head & 1), lax.axis_index("y"), (7 * head) >> 1]
    numbers = jnp.concatenate([jnp.stack(numbers).astype(i32), low])
    q = jnp.transpose(queries).reshape(HEADS, HEAD_DIM, ROWS)
    first, q = tie(first, q, ids, numbers, *maps)

    q = exchange(q)
    other = other_core(first)
    halo = lax.ppermute(cut(first, other), "z", following)
    inner, rows, params, bc = prep(numbers, first, other, ids, maps)
    keep = keeps(numbers, params, first, other, ids)

    late, late_states, left, acc, stat = attend_near(numbers, q, first, other, ids, rows, keep, bc)
    came = lax.ppermute(left, "z", following)
    halo = gate(halo, late_states)
    early, states = attend_far(
        numbers, q, halo, other_core(halo), ids, came, acc, stat, rows, keep, bc, late_states
    )
    mixed = scan(numbers, params, (early, late), inner, states, other_core(states), rows, keep, bc)
    return jnp.transpose(exchange(mixed).reshape(HEADS * HEAD_DIM, ROWS))


def solution(mesh):
    devices = mesh.devices.reshape(-1, 4, 4, 2)
    return jax.shard_map(
        on_device,
        mesh=Mesh(devices, ("z", "y", "x", "core")),
        in_specs=(
            P(("z", "y", "x", "core"), None),
            P(("z", "y", "x", "core"), None),
            P(("z", "y", "x", "core"), None),
            P(("z", "y", "x", "core"), None),
            P(("x", "core")),
            P(("x", "core")),
            P(("x", "core")),
            P(("z", "y"), None),
            P(("z", "y"), None),
            P(),
        ),
        out_specs=P(("z", "y", "x", "core"), None),
        check_vma=False,
    )
```

```python
import functools
import math

import jax
import jax.numpy as jnp
from jax import lax
from jax.experimental import pallas as pl
from jax.experimental.pallas import tpu as pltpu
from jax.sharding import Mesh
from jax.sharding import PartitionSpec as P

HEADS = 16
HEAD_DIM = 224
SSM_DIM = 64
STATE = 64
ROWS = 128
PLANE = 4096
REACH = 2048
CHUNKS = 16
SSM = 4
WIDE = SSM * SSM_DIM
KV = 480
FIRST = 496
LOG2E = math.log2(math.e)
NT = (((1,), (1,)), ((), ()))
VMEM_LIMIT = 20 * 1024 * 1024

VMEM = pl.BlockSpec(memory_space=pltpu.VMEM)
ANYWHERE = pl.BlockSpec(memory_space=pl.ANY)
SMEM = pl.BlockSpec(memory_space=pltpu.SMEM)
HBM = pl.BlockSpec(memory_space=pltpu.HBM)
CORE, OFFSET, Y_AT, FIRST_MAMBA, LOW = range(5)
NUMBERS = LOW + 4

f32, bf16, i32 = jnp.float32, jnp.bfloat16, jnp.int32


def in_hbm(x):
    return pltpu.with_memory_space_constraint(x, pltpu.HBM)


def in_vmem(x):
    return pltpu.with_memory_space_constraint(x, pltpu.VMEM)


def iota(shape, dim):
    return lax.broadcasted_iota(i32, shape, dim)


def spread(rows):
    width = rows.shape[-1]
    return jnp.concatenate(
        [jnp.broadcast_to(rows[r : r + 1, :], (SSM_DIM, width)) for r in range(SSM)], axis=0
    )


def parts(x):
    high = x.astype(bf16).astype(f32)
    mid = (x - high).astype(bf16).astype(f32)
    return high, mid, x - high - mid


def pack_first_kernel(
    bias_any, decay_any, skip_any, k_any, v_any, raw_any, out_any,
    k_ref, v_ref, raw_ref, out_ref, bias_ref, decay_ref, skip_ref, sems
):
    copies = []
    for step in range(4):
        at = pl.ds(896 * step, 896)
        copies.append(pltpu.make_async_copy(v_any.at[:, at], v_ref.at[step], sems.at[2 * step]))
        copies.append(pltpu.make_async_copy(k_any.at[:, at], k_ref.at[step], sems.at[2 * step + 1]))
    small = [
        pltpu.make_async_copy(have, need, sems.at[12 + n])
        for n, (have, need) in enumerate(
            ((raw_any, raw_ref), (bias_any, bias_ref), (decay_any, decay_ref), (skip_any, skip_ref))
        )
    ]
    start_all(small + copies)
    wait_all(small)
    lane = iota((1, ROWS), 1)
    whole = jnp.zeros((1, ROWS), f32)
    for n, ref in enumerate((bias_ref, decay_ref, skip_ref)):
        for j in range(7):
            whole = jnp.where(lane == 7 * n + j, ref[j], whole)
    high, mid, low = parts(whole)
    rr, jj = iota((256, 56), 0), iota((256, 56), 1)
    chosen = (((rr & 15) < SSM) & (jj == ((7 * (rr >> 4)) >> 1) + (rr & 15))).astype(bf16)
    rows = jnp.dot(chosen, raw_ref[...], preferred_element_type=f32)
    r = iota((256, ROWS), 0) & 15
    rows = jnp.where(r == 4, high, jnp.where(r == 5, mid, jnp.where(r == 6, low, rows))).astype(bf16)
    for h in range(HEADS):
        out_ref[h, 480:496, :] = rows[16 * h : 16 * h + 16, :]
    writes = []
    for step in range(4):
        wait_all(copies[2 * step : 2 * step + 2])
        vt = jnp.transpose(v_ref[step])
        for n in range(4):
            h = 4 * step + n
            k = k_ref[step, :, 224 * n : 224 * n + 224]
            out_ref[h, 0:128, :] = k[:, 0:128]
            out_ref[h, 128:256, :] = jnp.concatenate([k[:, 128:224], jnp.zeros((ROWS, 32), bf16)], axis=1)
            out_ref[h, 256:480, :] = vt[224 * n : 224 * n + 224, :]
        at = pl.ds(4 * step, 4)
        writes.append(pltpu.make_async_copy(out_ref.at[at], out_any.at[at], sems.at[8 + step]))
        writes[-1].start()
    wait_all(writes)


def pack_first(keys, values, raw, step_bias, decay_rate, skip_gain):
    return pl.pallas_call(
        pack_first_kernel,
        in_specs=[HBM] * 6,
        out_specs=HBM,
        out_shape=pltpu.HBM((HEADS, FIRST, ROWS), bf16),
        scratch_shapes=[
            pltpu.VMEM((4, ROWS, 896), bf16),
            pltpu.VMEM((4, ROWS, 896), bf16),
            pltpu.VMEM((56, ROWS), bf16),
            pltpu.VMEM((HEADS, FIRST, ROWS), bf16),
            pltpu.SMEM((7,), f32),
            pltpu.SMEM((7,), f32),
            pltpu.SMEM((7,), f32),
            pltpu.SemaphoreType.DMA((16,)),
        ],
        compiler_params=pltpu.CompilerParams(vmem_limit_bytes=VMEM_LIMIT),
        name="pack_keys_values",
    )(*(in_hbm(x) for x in (step_bias, decay_rate, skip_gain, keys, values, raw)))


def cut_kernel(first_ref, before_ref, out_ref):
    out_ref[...] = first_ref[8:16, 0:KV, :]


def cut(first, before):
    return pl.pallas_call(
        cut_kernel,
        in_specs=[VMEM, ANYWHERE],
        out_specs=VMEM,
        out_shape=jax.ShapeDtypeStruct((8, KV, ROWS), bf16),
        compiler_params=pltpu.CompilerParams(vmem_limit_bytes=VMEM_LIMIT),
        name="cut_halo",
    )(first, before)


def gate_kernel(*refs):
    pass


def gate(x, *before):
    return pl.pallas_call(
        gate_kernel,
        in_specs=[ANYWHERE] * (1 + len(before)),
        out_specs=ANYWHERE,
        out_shape=pltpu.VMEM(x.shape, x.dtype),
        input_output_aliases={0: 0},
        name="gate",
    )(in_vmem(x), *before)


def tie(first, q, *before):
    return pl.pallas_call(
        gate_kernel,
        in_specs=[ANYWHERE] * (2 + len(before)),
        out_specs=(ANYWHERE,) * 2,
        out_shape=(pltpu.VMEM(first.shape, first.dtype), jax.ShapeDtypeStruct(q.shape, q.dtype)),
        input_output_aliases={0: 0, 1: 1},
        name="tie",
    )(in_vmem(first), q, *before)


def step_sizes(raw, bias, decay):
    z = raw + bias
    dt = jnp.maximum(z, 0.0) + jnp.log1p(jnp.exp(-jnp.abs(z)))
    return dt, -dt * decay


def prep_kernel(
    num_ref, own_ref, other_ref, ds_ref, b0_ref, b1_ref, b2_ref, b3_ref, inner_ref, rows_ref, par_ref, bc_ref, sems
):
    core = num_ref[CORE]
    copies = [
        pltpu.make_async_copy(ref, bc_ref.at[pl.ds(4 * ((num_ref[Y_AT] - d) & 3), 4)], sems.at[d])
        for d, ref in enumerate((b0_ref, b1_ref, b2_ref, b3_ref))
    ]
    for copy in copies:
        copy.start()
    shape = (CHUNKS * 16, ROWS)
    line, lane = iota(shape, 0), iota(shape, 1)
    r = line & 15
    bias, decay = jnp.zeros(shape, f32), jnp.zeros(shape, f32)
    par_ref[...] = jnp.zeros_like(par_ref)
    for n in range(SSM):
        mamba = num_ref[FIRST_MAMBA] + n
        holder = (mamba * 37) >> 8
        at = mamba - 7 * holder
        held = jnp.where((holder & 1) == core, own_ref[holder >> 1], other_ref[holder >> 1]).astype(f32)
        held = held[4:5, :] + held[5:6, :] + held[6:7, :]

        def value(which):
            chosen = jnp.where(iota((1, ROWS), 1) == 7 * which + at, held, 0.0)
            return jnp.sum(chosen, axis=1, keepdims=True)

        for which in range(3):
            par_ref[4 * which + n : 4 * which + n + 1, :] = jnp.broadcast_to(value(which), (1, ROWS))
        bias = jnp.where(r == n, value(0), bias)
        decay = jnp.where(r == n, value(1), decay)
    upper = (iota((ROWS, ROWS), 0) <= iota((ROWS, ROWS), 1)).astype(f32)
    ids = spread_ids(ds_ref, 0)
    dt, log_step = step_sizes(own_ref[...].reshape(shape).astype(f32), bias, decay)
    running = jnp.dot(log_step, upper, precision=lax.Precision.HIGHEST, preferred_element_type=f32)
    start = 256 * (line >> 4) + 128 * core
    whole = jnp.broadcast_to(running[:, 127:128], shape)
    last = jnp.broadcast_to(ids[:, 127:128], shape)
    tail = jnp.where(start + lane >= last, jnp.exp(whole - running) * dt, 0.0)
    enter = jnp.where(ids < start, jnp.exp(running), 0.0)
    for b in range(CHUNKS):
        at = 16 * b
        rows_ref[b, 0:4, :] = tail[at : at + 4, :]
        rows_ref[b, 4:8, :] = enter[at : at + 4, :]
    running_t, dt_t = jnp.transpose(running), jnp.transpose(dt)
    s_at, t_at = iota((ROWS, ROWS), 0), iota((ROWS, ROWS), 1)
    for copy in copies:
        copy.wait()
    for b in range(CHUNKS):
        at = 16 * b
        state_in = jnp.transpose(bc_ref[b, 0:64, :].astype(f32)).astype(bf16)
        mix = jnp.dot(state_in, bc_ref[b, 64:128, :], preferred_element_type=f32)
        base = 256 * b + 128 * core
        allowed = (s_at <= t_at) & (s_at >= ids[at : at + 1, :] - base)
        for n in range(SSM):
            gap = running[at + n : at + n + 1, :] - running_t[:, at + n : at + n + 1]
            value = jnp.exp(jnp.where(allowed, gap, 0.0)) * mix * dt_t[:, at + n : at + n + 1]
            inner_ref[b, n, :, :] = jnp.where(allowed, value, 0.0).astype(bf16)


def spread_ids(ds_ref, which):
    return jnp.concatenate(
        [jnp.broadcast_to(ds_ref[b, which : which + 1, :], (16, ROWS)) for b in range(CHUNKS)], axis=0
    )


STEPS = pl.BlockSpec((CHUNKS, 16, ROWS), lambda i: (0, 30, 0))


def prep(numbers, own, other, ids, maps):
    return pl.pallas_call(
        prep_kernel,
        grid=(1,),
        in_specs=[SMEM, STEPS, STEPS, VMEM] + [ANYWHERE] * 4,
        out_shape=(
            jax.ShapeDtypeStruct((CHUNKS, SSM, ROWS, ROWS), bf16),
            jax.ShapeDtypeStruct((CHUNKS, 8, ROWS), f32),
            jax.ShapeDtypeStruct((16, ROWS), f32),
            jax.ShapeDtypeStruct((CHUNKS, 128, ROWS), bf16),
        ),
        out_specs=(VMEM,) * 4,
        scratch_shapes=[pltpu.SemaphoreType.DMA((4,))],
        compiler_params=pltpu.CompilerParams(vmem_limit_bytes=VMEM_LIMIT),
        cost_estimate=pl.CostEstimate(flops=200_000_000, bytes_accessed=8_000_000, transcendentals=2_000_000),
        name="scan_weights",
    )(numbers, own, other, ids, *maps)


def keep_kernel(num_ref, par_ref, own_ref, other_ref, ds_ref, keep_ref):
    core = num_ref[CORE]
    shape = (CHUNKS * 16, ROWS)
    line = iota(shape, 0)
    bias = jnp.concatenate([par_ref[0:4, :], jnp.zeros((12, ROWS), f32)] * CHUNKS, axis=0)
    decay = jnp.concatenate([par_ref[4:8, :], jnp.zeros((12, ROWS), f32)] * CHUNKS, axis=0)

    def keep(which):
        at = jnp.where(which == core, 0, 1)
        ids = jnp.where(at == 0, spread_ids(ds_ref, 0), spread_ids(ds_ref, 1))
        raw = jnp.where(at == 0, own_ref[...], other_ref[...]).reshape(shape).astype(f32)
        whole = jnp.sum(step_sizes(raw, bias, decay)[1], axis=1, keepdims=True)
        value = jnp.where(ids[:, 127:128] < 256 * (line[:, 0:1] >> 4) + 128 * which, jnp.exp(whole), 0.0)
        return jnp.broadcast_to(value, shape)

    for which in range(2):
        kept = keep(which)
        for b in range(CHUNKS):
            keep_ref[b, 4 * which : 4 * which + 4, :] = kept[16 * b : 16 * b + 4, :]


def keeps(numbers, params, own, other, ids):
    return pl.pallas_call(
        keep_kernel,
        grid=(1,),
        in_specs=[SMEM, VMEM, STEPS, STEPS, VMEM],
        out_specs=VMEM,
        out_shape=jax.ShapeDtypeStruct((CHUNKS, 8, ROWS), f32),
        compiler_params=pltpu.CompilerParams(vmem_limit_bytes=VMEM_LIMIT),
        name="scan_keeps",
    )(numbers, params, own, other, ids)


class Tiles:
    def __init__(self, core, shift, own, other, q, ds, scratch):
        self.core, self.shift, self.refs, self.q, self.ds = core, shift, (own, other), q, ds
        self.even, self.odd, self.turned = scratch

    def start(self, tile):
        for n in range(4):
            self.turned[0:HEAD_DIM, 128 * n : 128 * n + 128] = self.q[4 * tile + n]
        self.turned[HEAD_DIM:256, :] = jnp.zeros((32, 512), bf16)
        self.ids = jnp.concatenate([self.ds[4 * tile + n, 0:1, :] for n in range(4)], axis=1)
        lane = iota((1, 512), 1)
        self.q_at = 1024 * tile + 128 * self.core + (lane & 127) + 256 * (lane >> 7)

    def score(self, p, s, lanes=slice(0, 512)):
        k = jnp.concatenate(
            [
                jnp.concatenate([ref[2 * p + j, 0:128, :], ref[2 * p + j, 128:256, :]], axis=1)
                for j in range(2)
                for ref in self.refs
            ],
            axis=0,
        )
        s[:, lanes] = jnp.dot(k, self.turned[:, lanes], preferred_element_type=f32)

    def absorb(self, p, s, acc_ref, stat_ref, lanes=slice(0, 512), causal=False, valid=True):
        width = lanes.stop - lanes.start
        scale = LOG2E / math.sqrt(HEAD_DIM)
        line = iota((ROWS, width), 0)
        ids = jnp.where(valid, self.ids[:, lanes], 1 << 20)
        pieces = []
        for j in range(4):
            at = 512 * p + self.shift + 256 * (j // 2) + 128 * (self.core if j % 2 == 0 else 1 - self.core)
            allowed = line >= ids - at
            if causal:
                allowed = allowed & (line <= self.q_at[:, lanes] - at)
            pieces.append(jnp.where(allowed, s[128 * j : 128 * j + 128, lanes], -1e30))
        masked = jnp.concatenate(pieces, axis=0)
        top = stat_ref[0:1, lanes]
        new_top = jnp.maximum(top, jnp.max(masked, axis=0, keepdims=True))
        expo = jnp.exp2((masked - new_top) * scale)
        fade = jnp.exp2((top - new_top) * scale)
        stat_ref[1:2, lanes] = stat_ref[1:2, lanes] * fade + jnp.sum(expo, axis=0, keepdims=True)
        stat_ref[0:1, lanes] = new_top
        v = jnp.concatenate([ref[2 * p + j, 256:480, :] for j in range(2) for ref in self.refs], axis=1)
        acc_ref[:, lanes] = acc_ref[:, lanes] * fade + jnp.dot(v, expo.astype(bf16), preferred_element_type=f32)

    def back(self, p, low, acc_ref, stat_ref):
        def two(n, carry):
            at = p - 2 * n
            self.score(jnp.maximum(at - 1, 0), self.odd)
            self.absorb(at, self.even, acc_ref, stat_ref)
            self.score(jnp.maximum(at - 2, 0), self.even)
            self.absorb(jnp.maximum(at - 1, 0), self.odd, acc_ref, stat_ref, valid=at - 1 >= low)
            return carry

        lax.fori_loop(0, jnp.maximum(p - low + 2, 0) >> 1, two, 0)


def own_states(x_ref, rows_ref, keep_ref, maps_ref, send_ref, core):
    total = jnp.zeros((WIDE, STATE), f32)
    for pair in range(4):
        states = []
        for b in (2 * pair, 2 * pair + 1):
            weighted = (x_ref[b].astype(f32) * spread(rows_ref[b, 0:4, :])).astype(bf16)
            state = lax.dot_general(weighted, maps_ref[b, 0:64, :], NT, preferred_element_type=f32)
            states.append(state)
            first, second = spread(keep_ref[b, 0:4, 0:64]), spread(keep_ref[b, 4:8, 0:64])
            total = (first * second) * total + jnp.where(core == 0, second, 1.0) * state
        send_ref[pair] = jnp.concatenate(states, axis=1).astype(bf16)
    return total


def start_all(copies):
    for copy in copies:
        copy.start()


def wait_all(copies):
    for copy in copies:
        copy.wait()


def put_x(x_ref, at, off, acc, total):
    x = (acc / total).astype(bf16)
    for n in range(4):
        x_ref[at + n, pl.ds(off, HEAD_DIM), :] = x[:, 128 * n : 128 * n + 128]


def near_kernel(
    num_any, q_ref, own_ref, other_ref, ds_ref, rows_any, keep_any, maps_any,
    x_out, send_out, left_ref, acc_out, stat_out,
    even, odd, even_2, odd_2, turned, turned_2, acc_ref, stat_ref, x_ref, send_ref, rows_ref, keep_ref, maps_ref, num_ref, sems,
):
    numbers = pltpu.make_async_copy(num_any, num_ref, sems.at[3])
    numbers.start()
    reads = [
        pltpu.make_async_copy(ref.at[pl.ds(8, 8)], to, sems.at[n])
        for n, (ref, to) in enumerate(((rows_any, rows_ref), (keep_any, keep_ref), (maps_any, maps_ref)))
    ]
    start_all(reads)
    acc_ref[...] = jnp.zeros_like(acc_ref)
    stat_ref[...] = jnp.where(iota(stat_ref.shape, 1) == 0, -1e30, 0.0)
    writes = [
        pltpu.make_async_copy(acc_ref.at[pl.ds(0, 2)], acc_out, sems.at[4]),
        pltpu.make_async_copy(stat_ref.at[pl.ds(0, 2)], stat_out, sems.at[5]),
        pltpu.make_async_copy(x_ref, x_out, sems.at[6]),
        pltpu.make_async_copy(send_ref, send_out, sems.at[7]),
    ]
    core = lax.axis_index("core")
    sets = [
        Tiles(core, 0, own_ref, other_ref, q_ref, ds_ref, scratch)
        for scratch in ((even, odd, turned), (even_2, odd_2, turned_2))
    ]
    late = slice(256, 512)

    def state_of(i):
        return acc_ref.at[i], stat_ref.at[i]

    def begin(i):
        tiles = sets[i % 2]
        tiles.start(i)
        tiles.score(2 * i + 1, tiles.odd, late)
        tiles.score(2 * i, tiles.even)

    begin(0)
    for i in range(4):
        if i < 3:
            begin(i + 1)
        tiles = sets[i % 2]
        tiles.absorb(2 * i + 1, tiles.odd, *state_of(i), late, causal=True)
        tiles.absorb(2 * i, tiles.even, *state_of(i), causal=True)
    numbers.wait()
    off = pl.multiple_of(num_ref[OFFSET], 32)
    x_ref[...] = jnp.zeros_like(x_ref)
    for i in range(1, 4):
        tiles = sets[i % 2]
        tiles.start(i)
        tiles.score(2 * i - 1, tiles.even)
        tiles.back(2 * i - 1, jnp.maximum(num_ref[LOW + i], 0), *state_of(i))
        if i == 1:
            start_all(writes[0:2])
        else:
            put_x(x_ref, 4 * i - 8, off, acc_ref[i], stat_ref[i, 1:2, :])
    start_all(writes[2:3])
    wait_all(reads)
    total = own_states(x_ref, rows_ref, keep_ref, maps_ref, send_ref, core)
    start_all(writes[3:4])
    left_ref[...] = jnp.concatenate([total[0:128, :], total[128:256, :]], axis=1).astype(bf16)
    wait_all(writes)


STATE_BUFFERS = [
    pltpu.VMEM((8, 8, ROWS), f32),
    pltpu.VMEM((8, 8, ROWS), f32),
    pltpu.VMEM((8, 128, ROWS), bf16),
]


def attend_near(numbers, q, own, other, ids, rows, keep, maps):
    return pl.pallas_call(
        near_kernel,
        in_specs=[HBM] + [VMEM] * 4 + [HBM] * 3,
        out_specs=(HBM, HBM, VMEM, HBM, HBM),
        out_shape=(
            pltpu.HBM((8, WIDE, ROWS), bf16),
            pltpu.HBM((4, WIDE, 128), bf16),
            jax.ShapeDtypeStruct((128, 128), bf16),
            pltpu.HBM((2, HEAD_DIM, 512), f32),
            pltpu.HBM((2, 8, 512), f32),
        ),
        scratch_shapes=[pltpu.VMEM((512, 512), f32)] * 4
        + [pltpu.VMEM((256, 512), bf16)] * 2
        + [pltpu.VMEM((4, HEAD_DIM, 512), f32), pltpu.VMEM((4, 8, 512), f32)]
        + [pltpu.VMEM((8, WIDE, ROWS), bf16), pltpu.VMEM((4, WIDE, 128), bf16)]
        + STATE_BUFFERS
        + [pltpu.SMEM((NUMBERS,), i32), pltpu.SemaphoreType.DMA((8,))],
        compiler_params=pltpu.CompilerParams(vmem_limit_bytes=VMEM_LIMIT),
        cost_estimate=pl.CostEstimate(flops=5_000_000_000, bytes_accessed=9_000_000, transcendentals=4_000_000),
        name="attend_near",
    )(in_hbm(numbers), q, own, other, ids, in_hbm(rows), in_hbm(keep), in_hbm(maps))


def far_kernel(
    num_any, q_ref, own_ref, other_ref, ds_ref, came_ref, acc_any, stat_any, late_any, rows_any, keep_any, maps_any,
    x_ref, send_ref, even, odd, turned, acc_ref, stat_ref, near_acc, near_stat, rows_ref, keep_ref, maps_ref, num_ref, sems,
):
    reads = [
        pltpu.make_async_copy(num_any, num_ref, sems.at[0]),
        pltpu.make_async_copy(rows_any.at[pl.ds(0, 8)], rows_ref, sems.at[1]),
        pltpu.make_async_copy(keep_any.at[pl.ds(0, 8)], keep_ref, sems.at[2]),
        pltpu.make_async_copy(maps_any.at[pl.ds(0, 8)], maps_ref, sems.at[3]),
    ]
    reads[1:1] = [
        pltpu.make_async_copy(acc_any, near_acc, sems.at[4]),
        pltpu.make_async_copy(stat_any, near_stat, sems.at[5]),
    ]
    reads.append(pltpu.make_async_copy(late_any, send_ref.at[pl.ds(4, 4)], sems.at[6]))
    start_all(reads)
    x_ref[...] = jnp.zeros_like(x_ref)
    send_ref[8, 0:128, :] = came_ref[...]
    send_ref[8, 128:256, :] = jnp.zeros((128, 128), bf16)
    acc_ref[...] = jnp.zeros_like(acc_ref)
    stat_ref[...] = jnp.where(iota(stat_ref.shape, 1) == 0, -1e30, 0.0)
    core = lax.axis_index("core")
    tiles = Tiles(core, -REACH, own_ref, other_ref, q_ref, ds_ref, (even, odd, turned))
    tiles.start(0)
    tiles.score(3, even)
    wait_all(reads[0:1])
    off = pl.multiple_of(num_ref[OFFSET], 32)
    for i in range(2):
        low = jnp.clip(num_ref[LOW + i] + 4, 0, 4)

        @pl.when(low < 4)
        def _():
            if i > 0:
                tiles.start(i)
                tiles.score(3, even)
            tiles.back(3, low, acc_ref.at[i], stat_ref.at[i])

    wait_all(reads[1:3])
    scale = LOG2E / math.sqrt(HEAD_DIM)
    for i in range(2):
        top = jnp.maximum(near_stat[i, 0:1, :], stat_ref[i, 0:1, :])
        near = jnp.exp2((near_stat[i, 0:1, :] - top) * scale)
        far = jnp.exp2((stat_ref[i, 0:1, :] - top) * scale)
        total = near_stat[i, 1:2, :] * near + stat_ref[i, 1:2, :] * far
        put_x(x_ref, 4 * i, off, near_acc[i] * near + acc_ref[i] * far, total)
    wait_all(reads[3:])
    own_states(x_ref, rows_ref, keep_ref, maps_ref, send_ref, core)


def attend_far(numbers, q, own, other, ids, came, acc, stat, rows, keep, maps, late_states):
    return pl.pallas_call(
        far_kernel,
        in_specs=[HBM] + [VMEM] * 5 + [HBM] * 6,
        out_specs=(VMEM,) * 2,
        out_shape=(
            jax.ShapeDtypeStruct((8, WIDE, ROWS), bf16),
            jax.ShapeDtypeStruct((9, WIDE, 128), bf16),
        ),
        scratch_shapes=[pltpu.VMEM((512, 512), f32)] * 2
        + [pltpu.VMEM((256, 512), bf16)]
        + [pltpu.VMEM((2, HEAD_DIM, 512), f32), pltpu.VMEM((2, 8, 512), f32)] * 2
        + STATE_BUFFERS
        + [pltpu.SMEM((NUMBERS,), i32), pltpu.SemaphoreType.DMA((7,))],
        compiler_params=pltpu.CompilerParams(vmem_limit_bytes=VMEM_LIMIT),
        cost_estimate=pl.CostEstimate(flops=2_000_000_000, bytes_accessed=5_000_000, transcendentals=1_000_000),
        name="attend_far",
    )(
        in_hbm(numbers), q, in_vmem(own), other, ids, came, in_hbm(acc), in_hbm(stat), in_hbm(late_states),
        in_hbm(rows), in_hbm(keep), in_hbm(maps),
    )


def scan_kernel(
    num_ref, par_ref, xe_ref, xl_ref, inner_ref, own_ref, other_ref, f_ref, g_ref, rows_ref, keep_ref, bc_ref,
    out_ref, state_ref, hold,
):
    step = pl.program_id(0)
    core, off = num_ref[CORE], pl.multiple_of(num_ref[OFFSET], 32)
    early = step < 2

    @pl.when(step == 0)
    def _():
        packed = f_ref[0, 0:128, :].astype(f32) + g_ref[0, 0:128, :].astype(f32)
        state_ref[0:128, :] = packed[:, 0:64]
        state_ref[128:256, :] = packed[:, 64:128]

    state = state_ref[...]
    for b in range(4):
        at = slice(64 * (b % 2), 64 * (b % 2) + 64)
        mine, theirs = own_ref[b // 2, :, at].astype(f32), other_ref[b // 2, :, at].astype(f32)
        first, second = spread(keep_ref[b, 0:4, 0:64]), spread(keep_ref[b, 4:8, 0:64])
        middle = first * state + jnp.where(core == 0, mine, theirs)
        entering = jnp.where(core == 0, state, middle).astype(bf16)
        state = second * middle + jnp.where(core == 0, theirs, mine)
        carried = jnp.dot(entering, bc_ref[b, 64:128, :], preferred_element_type=f32)
        enter = rows_ref[b, 4:8, :]
        for n in range(SSM):
            rows = slice(64 * n, 64 * n + 64)
            x = jnp.where(early, xe_ref[b, rows, :], xl_ref[b, rows, :])
            y = jnp.dot(x, inner_ref[b, n], preferred_element_type=f32)
            hold[b, rows, :] = y + par_ref[8 + n : 9 + n, :] * x.astype(f32) + carried[rows] * enter[n : n + 1, :]
        out_ref[b] = hold[b, pl.ds(off, HEAD_DIM), :].astype(bf16)
    state_ref[...] = state


def scan(numbers, params, x, inner, own, other, rows, keep, maps):
    def chunks(*shape):
        return pl.BlockSpec(shape, lambda i: (i,) + (0,) * (len(shape) - 1))

    def halves(*shape):
        zeros = (0,) * (len(shape) - 1)
        return [
            pl.BlockSpec(shape, lambda i: (jnp.minimum(i, 1),) + zeros),
            pl.BlockSpec(shape, lambda i: (jnp.maximum(i - 2, 0),) + zeros),
        ]

    return pl.pallas_call(
        scan_kernel,
        grid=(4,),
        in_specs=[SMEM, pl.BlockSpec((16, ROWS), lambda i: (0, 0))]
        + halves(4, WIDE, ROWS)
        + [chunks(4, SSM, ROWS, ROWS)]
        + [chunks(2, WIDE, 128)] * 2
        + [pl.BlockSpec((1, WIDE, 128), lambda i: (8, 0, 0))] * 2
        + [chunks(4, 8, ROWS), chunks(4, 8, ROWS), chunks(4, 128, ROWS)],
        out_specs=chunks(4, HEAD_DIM, ROWS),
        out_shape=jax.ShapeDtypeStruct((CHUNKS, HEAD_DIM, ROWS), bf16),
        scratch_shapes=[pltpu.VMEM((WIDE, STATE), f32), pltpu.VMEM((4, WIDE, ROWS), f32)],
        compiler_params=pltpu.CompilerParams(vmem_limit_bytes=VMEM_LIMIT),
        name="scan",
    )(numbers, params, *x, inner, own, other, own, other, rows, keep, maps)


def other_core(x):
    return lax.ppermute(x, "core", [(0, 1), (1, 0)])


def exchange(x):
    return lax.all_to_all(x, ("y", "x"), split_axis=0, concat_axis=0, tiled=True)


def document_starts(segment_ids, plane):
    padded = jnp.concatenate([jnp.full((REACH + 1,), -1, i32), segment_ids])
    window = lax.dynamic_slice_in_dim(padded, plane * PLANE, PLANE + REACH + 1, 0)
    place = jnp.arange(PLANE + REACH, dtype=i32) - REACH
    starts = jnp.where(window[1:] != window[:-1], place, -REACH).reshape(48, 128)
    within = lax.cummax(starts, axis=1)
    before = lax.cummax(within[:, 127], axis=0)
    before = jnp.concatenate([jnp.full((1,), -REACH, i32), before[:-1]])
    return jnp.maximum(within, before[:, None])[16:]


def on_device(
    queries, keys, values, step_raw, step_bias, decay_rate, skip_gain, state_in, state_out, segment_ids
):
    core, planes = lax.axis_index("core"), lax.axis_size("z")
    plane, head = lax.axis_index("z"), 4 * lax.axis_index("y") + lax.axis_index("x")
    following = [(i, i + 1) for i in range(planes - 1)]

    first = exchange(pack_first(keys, values, jnp.transpose(step_raw), step_bias, decay_rate, skip_gain))
    both = jnp.concatenate([jnp.transpose(state_in), jnp.transpose(state_out)], axis=0).reshape(128, 4, 2, ROWS)
    both = jnp.transpose(lax.dynamic_index_in_dim(both, core, 2, keepdims=False), (1, 0, 2))
    maps = [both] + [lax.ppermute(both, "y", [(i, (i + d) % 4) for i in range(4)]) for d in range(1, 4)]

    starts = document_starts(segment_ids, plane).reshape(CHUNKS, 2, ROWS)
    ids = jnp.where(core == 0, starts, starts[:, ::-1])
    low = ids[0::4, 0, 0] >> 9
    numbers = [core, 32 * (head & 1), lax.axis_index("y"), (7 * head) >> 1]
    numbers = jnp.concatenate([jnp.stack(numbers).astype(i32), low])
    q = jnp.transpose(queries).reshape(HEADS, HEAD_DIM, ROWS)
    first, q = tie(first, q, ids, numbers, *maps)

    q = exchange(q)
    other = other_core(first)
    halo = lax.ppermute(cut(first, other), "z", following)
    inner, rows, params, bc = prep(numbers, first, other, ids, maps)
    keep = keeps(numbers, params, first, other, ids)

    late, late_states, left, acc, stat = attend_near(numbers, q, first, other, ids, rows, keep, bc)
    came = lax.ppermute(left, "z", following)
    halo = gate(halo, late_states)
    early, states = attend_far(
        numbers, q, halo, other_core(halo), ids, came, acc, stat, rows, keep, bc, late_states
    )
    mixed = scan(numbers, params, (early, late), inner, states, other_core(states), rows, keep, bc)
    return jnp.transpose(exchange(mixed).reshape(HEADS * HEAD_DIM, ROWS))


def solution(mesh):
    devices = mesh.devices.reshape(-1, 4, 4, 2)
    return jax.shard_map(
        on_device,
        mesh=Mesh(devices, ("z", "y", "x", "core")),
        in_specs=(
            P(("z", "y", "x", "core"), None),
            P(("z", "y", "x", "core"), None),
            P(("z", "y", "x", "core"), None),
            P(("z", "y", "x", "core"), None),
            P(("x", "core")),
            P(("x", "core")),
            P(("x", "core")),
            P(("z", "y"), None),
            P(("z", "y"), None),
            P(),
        ),
        out_specs=P(("z", "y", "x", "core"), None),
        check_vma=False,
    )
```

```python
import functools
import math

import jax
import jax.numpy as jnp
from jax import lax
from jax.experimental import pallas as pl
from jax.experimental.pallas import tpu as pltpu
from jax.sharding import Mesh
from jax.sharding import PartitionSpec as P

HEADS = 16
HEAD_DIM = 224
SSM_DIM = 64
STATE = 64
ROWS = 128
PLANE = 4096
REACH = 2048
CHUNKS = 16
SSM = 4
WIDE = SSM * SSM_DIM
KV = 480
FIRST = 496
LOG2E = math.log2(math.e)
NT = (((1,), (1,)), ((), ()))
VMEM_LIMIT = 20 * 1024 * 1024

VMEM = pl.BlockSpec(memory_space=pltpu.VMEM)
ANYWHERE = pl.BlockSpec(memory_space=pl.ANY)
SMEM = pl.BlockSpec(memory_space=pltpu.SMEM)
HBM = pl.BlockSpec(memory_space=pltpu.HBM)
CORE, OFFSET, Y_AT, FIRST_MAMBA, LOW = range(5)
NUMBERS = LOW + 4

f32, bf16, i32 = jnp.float32, jnp.bfloat16, jnp.int32


def in_hbm(x):
    return pltpu.with_memory_space_constraint(x, pltpu.HBM)


def in_vmem(x):
    return pltpu.with_memory_space_constraint(x, pltpu.VMEM)


def iota(shape, dim):
    return lax.broadcasted_iota(i32, shape, dim)


def spread(rows):
    width = rows.shape[-1]
    return jnp.concatenate(
        [jnp.broadcast_to(rows[r : r + 1, :], (SSM_DIM, width)) for r in range(SSM)], axis=0
    )


def parts(x):
    high = x.astype(bf16).astype(f32)
    mid = (x - high).astype(bf16).astype(f32)
    return high, mid, x - high - mid


def pack_first_kernel(
    bias_any, decay_any, skip_any, k_any, v_any, raw_any, out_any,
    k_ref, v_ref, raw_ref, out_ref, bias_ref, decay_ref, skip_ref, sems
):
    copies = []
    for step in range(4):
        at = pl.ds(896 * step, 896)
        copies.append(pltpu.make_async_copy(v_any.at[:, at], v_ref.at[step], sems.at[2 * step]))
        copies.append(pltpu.make_async_copy(k_any.at[:, at], k_ref.at[step], sems.at[2 * step + 1]))
    small = [
        pltpu.make_async_copy(have, need, sems.at[12 + n])
        for n, (have, need) in enumerate(
            ((raw_any, raw_ref), (bias_any, bias_ref), (decay_any, decay_ref), (skip_any, skip_ref))
        )
    ]
    start_all(small + copies)
    wait_all(small)
    lane = iota((1, ROWS), 1)
    whole = jnp.zeros((1, ROWS), f32)
    for n, ref in enumerate((bias_ref, decay_ref, skip_ref)):
        for j in range(7):
            whole = jnp.where(lane == 7 * n + j, ref[j], whole)
    high, mid, low = parts(whole)
    rr, jj = iota((256, 56), 0), iota((256, 56), 1)
    chosen = (((rr & 15) < SSM) & (jj == ((7 * (rr >> 4)) >> 1) + (rr & 15))).astype(bf16)
    rows = jnp.dot(chosen, raw_ref[...], preferred_element_type=f32)
    r = iota((256, ROWS), 0) & 15
    rows = jnp.where(r == 4, high, jnp.where(r == 5, mid, jnp.where(r == 6, low, rows))).astype(bf16)
    for h in range(HEADS):
        out_ref[h, 480:496, :] = rows[16 * h : 16 * h + 16, :]
    writes = []
    for step in range(4):
        wait_all(copies[2 * step : 2 * step + 2])
        vt = jnp.transpose(v_ref[step])
        for n in range(4):
            h = 4 * step + n
            k = k_ref[step, :, 224 * n : 224 * n + 224]
            out_ref[h, 0:128, :] = k[:, 0:128]
            out_ref[h, 128:256, :] = jnp.concatenate([k[:, 128:224], jnp.zeros((ROWS, 32), bf16)], axis=1)
            out_ref[h, 256:480, :] = vt[224 * n : 224 * n + 224, :]
        at = pl.ds(4 * step, 4)
        writes.append(pltpu.make_async_copy(out_ref.at[at], out_any.at[at], sems.at[8 + step]))
        writes[-1].start()
    wait_all(writes)


def pack_first(keys, values, raw, step_bias, decay_rate, skip_gain):
    return pl.pallas_call(
        pack_first_kernel,
        in_specs=[HBM] * 6,
        out_specs=HBM,
        out_shape=pltpu.HBM((HEADS, FIRST, ROWS), bf16),
        scratch_shapes=[
            pltpu.VMEM((4, ROWS, 896), bf16),
            pltpu.VMEM((4, ROWS, 896), bf16),
            pltpu.VMEM((56, ROWS), bf16),
            pltpu.VMEM((HEADS, FIRST, ROWS), bf16),
            pltpu.SMEM((7,), f32),
            pltpu.SMEM((7,), f32),
            pltpu.SMEM((7,), f32),
            pltpu.SemaphoreType.DMA((16,)),
        ],
        compiler_params=pltpu.CompilerParams(vmem_limit_bytes=VMEM_LIMIT),
        name="pack_keys_values",
    )(*(in_hbm(x) for x in (step_bias, decay_rate, skip_gain, keys, values, raw)))


def cut_kernel(first_ref, before_ref, out_ref):
    out_ref[...] = first_ref[8:16, 0:KV, :]


def cut(first, before):
    return pl.pallas_call(
        cut_kernel,
        in_specs=[VMEM, ANYWHERE],
        out_specs=VMEM,
        out_shape=jax.ShapeDtypeStruct((8, KV, ROWS), bf16),
        compiler_params=pltpu.CompilerParams(vmem_limit_bytes=VMEM_LIMIT),
        name="cut_halo",
    )(first, before)


def gate_kernel(*refs):
    pass


def gate(x, *before):
    return pl.pallas_call(
        gate_kernel,
        in_specs=[ANYWHERE] * (1 + len(before)),
        out_specs=ANYWHERE,
        out_shape=pltpu.VMEM(x.shape, x.dtype),
        input_output_aliases={0: 0},
        name="gate",
    )(in_vmem(x), *before)


def tie(first, q, *before):
    return pl.pallas_call(
        gate_kernel,
        in_specs=[ANYWHERE] * (2 + len(before)),
        out_specs=(ANYWHERE,) * 2,
        out_shape=(pltpu.VMEM(first.shape, first.dtype), jax.ShapeDtypeStruct(q.shape, q.dtype)),
        input_output_aliases={0: 0, 1: 1},
        name="tie",
    )(in_vmem(first), q, *before)


def step_sizes(raw, bias, decay):
    z = raw + bias
    dt = jnp.maximum(z, 0.0) + jnp.log1p(jnp.exp(-jnp.abs(z)))
    return dt, -dt * decay


def prep_kernel(
    num_ref, own_ref, other_ref, ds_ref, b0_ref, b1_ref, b2_ref, b3_ref, inner_ref, rows_ref, par_ref, bc_ref, sems
):
    core = num_ref[CORE]
    copies = [
        pltpu.make_async_copy(ref, bc_ref.at[pl.ds(4 * ((num_ref[Y_AT] - d) & 3), 4)], sems.at[d])
        for d, ref in enumerate((b0_ref, b1_ref, b2_ref, b3_ref))
    ]
    for copy in copies:
        copy.start()
    shape = (CHUNKS * 16, ROWS)
    line, lane = iota(shape, 0), iota(shape, 1)
    r = line & 15
    bias, decay = jnp.zeros(shape, f32), jnp.zeros(shape, f32)
    par_ref[...] = jnp.zeros_like(par_ref)
    for n in range(SSM):
        mamba = num_ref[FIRST_MAMBA] + n
        holder = (mamba * 37) >> 8
        at = mamba - 7 * holder
        held = jnp.where((holder & 1) == core, own_ref[holder >> 1], other_ref[holder >> 1]).astype(f32)
        held = held[4:5, :] + held[5:6, :] + held[6:7, :]

        def value(which):
            chosen = jnp.where(iota((1, ROWS), 1) == 7 * which + at, held, 0.0)
            return jnp.sum(chosen, axis=1, keepdims=True)

        for which in range(3):
            par_ref[4 * which + n : 4 * which + n + 1, :] = jnp.broadcast_to(value(which), (1, ROWS))
        bias = jnp.where(r == n, value(0), bias)
        decay = jnp.where(r == n, value(1), decay)
    upper = (iota((ROWS, ROWS), 0) <= iota((ROWS, ROWS), 1)).astype(f32)
    ids = spread_ids(ds_ref, 0)
    dt, log_step = step_sizes(own_ref[...].reshape(shape).astype(f32), bias, decay)
    running = jnp.dot(log_step, upper, precision=lax.Precision.HIGHEST, preferred_element_type=f32)
    start = 256 * (line >> 4) + 128 * core
    whole = jnp.broadcast_to(running[:, 127:128], shape)
    last = jnp.broadcast_to(ids[:, 127:128], shape)
    tail = jnp.where(start + lane >= last, jnp.exp(whole - running) * dt, 0.0)
    enter = jnp.where(ids < start, jnp.exp(running), 0.0)
    for b in range(CHUNKS):
        at = 16 * b
        rows_ref[b, 0:4, :] = tail[at : at + 4, :]
        rows_ref[b, 4:8, :] = enter[at : at + 4, :]
    running_t, dt_t = jnp.transpose(running), jnp.transpose(dt)
    s_at, t_at = iota((ROWS, ROWS), 0), iota((ROWS, ROWS), 1)
    for copy in copies:
        copy.wait()
    for b in range(CHUNKS):
        at = 16 * b
        state_in = jnp.transpose(bc_ref[b, 0:64, :].astype(f32)).astype(bf16)
        mix = jnp.dot(state_in, bc_ref[b, 64:128, :], preferred_element_type=f32)
        base = 256 * b + 128 * core
        allowed = (s_at <= t_at) & (s_at >= ids[at : at + 1, :] - base)
        for n in range(SSM):
            gap = running[at + n : at + n + 1, :] - running_t[:, at + n : at + n + 1]
            value = jnp.exp(jnp.where(allowed, gap, 0.0)) * mix * dt_t[:, at + n : at + n + 1]
            inner_ref[b, n, :, :] = jnp.where(allowed, value, 0.0).astype(bf16)


def spread_ids(ds_ref, which):
    return jnp.concatenate(
        [jnp.broadcast_to(ds_ref[b, which : which + 1, :], (16, ROWS)) for b in range(CHUNKS)], axis=0
    )


STEPS = pl.BlockSpec((CHUNKS, 16, ROWS), lambda i: (0, 30, 0))


def prep(numbers, own, other, ids, maps):
    return pl.pallas_call(
        prep_kernel,
        grid=(1,),
        in_specs=[SMEM, STEPS, STEPS, VMEM] + [ANYWHERE] * 4,
        out_shape=(
            jax.ShapeDtypeStruct((CHUNKS, SSM, ROWS, ROWS), bf16),
            jax.ShapeDtypeStruct((CHUNKS, 8, ROWS), f32),
            jax.ShapeDtypeStruct((16, ROWS), f32),
            jax.ShapeDtypeStruct((CHUNKS, 128, ROWS), bf16),
        ),
        out_specs=(VMEM,) * 4,
        scratch_shapes=[pltpu.SemaphoreType.DMA((4,))],
        compiler_params=pltpu.CompilerParams(vmem_limit_bytes=VMEM_LIMIT),
        cost_estimate=pl.CostEstimate(flops=200_000_000, bytes_accessed=8_000_000, transcendentals=2_000_000),
        name="scan_weights",
    )(numbers, own, other, ids, *maps)


def keep_kernel(num_ref, par_ref, own_ref, other_ref, ds_ref, keep_ref):
    core = num_ref[CORE]
    shape = (CHUNKS * 16, ROWS)
    line = iota(shape, 0)
    bias = jnp.concatenate([par_ref[0:4, :], jnp.zeros((12, ROWS), f32)] * CHUNKS, axis=0)
    decay = jnp.concatenate([par_ref[4:8, :], jnp.zeros((12, ROWS), f32)] * CHUNKS, axis=0)

    def keep(which):
        at = jnp.where(which == core, 0, 1)
        ids = jnp.where(at == 0, spread_ids(ds_ref, 0), spread_ids(ds_ref, 1))
        raw = jnp.where(at == 0, own_ref[...], other_ref[...]).reshape(shape).astype(f32)
        whole = jnp.sum(step_sizes(raw, bias, decay)[1], axis=1, keepdims=True)
        value = jnp.where(ids[:, 127:128] < 256 * (line[:, 0:1] >> 4) + 128 * which, jnp.exp(whole), 0.0)
        return jnp.broadcast_to(value, shape)

    for which in range(2):
        kept = keep(which)
        for b in range(CHUNKS):
            keep_ref[b, 4 * which : 4 * which + 4, :] = kept[16 * b : 16 * b + 4, :]


def keeps(numbers, params, own, other, ids):
    return pl.pallas_call(
        keep_kernel,
        grid=(1,),
        in_specs=[SMEM, VMEM, STEPS, STEPS, VMEM],
        out_specs=VMEM,
        out_shape=jax.ShapeDtypeStruct((CHUNKS, 8, ROWS), f32),
        compiler_params=pltpu.CompilerParams(vmem_limit_bytes=VMEM_LIMIT),
        name="scan_keeps",
    )(numbers, params, own, other, ids)


class Tiles:
    def __init__(self, core, shift, own, other, q, ds, scratch):
        self.core, self.shift, self.refs, self.q, self.ds = core, shift, (own, other), q, ds
        self.even, self.odd, self.turned = scratch

    def start(self, tile):
        for n in range(4):
            self.turned[0:HEAD_DIM, 128 * n : 128 * n + 128] = self.q[4 * tile + n]
        self.turned[HEAD_DIM:256, :] = jnp.zeros((32, 512), bf16)
        self.ids = jnp.concatenate([self.ds[4 * tile + n, 0:1, :] for n in range(4)], axis=1)
        lane = iota((1, 512), 1)
        self.q_at = 1024 * tile + 128 * self.core + (lane & 127) + 256 * (lane >> 7)

    def score(self, p, s, lanes=slice(0, 512)):
        k = jnp.concatenate(
            [
                jnp.concatenate([ref[2 * p + j, 0:128, :], ref[2 * p + j, 128:256, :]], axis=1)
                for j in range(2)
                for ref in self.refs
            ],
            axis=0,
        )
        s[:, lanes] = jnp.dot(k, self.turned[:, lanes], preferred_element_type=f32)

    def absorb(self, p, s, acc_ref, stat_ref, lanes=slice(0, 512), causal=False):
        width = lanes.stop - lanes.start
        scale = LOG2E / math.sqrt(HEAD_DIM)
        line = iota((ROWS, width), 0)
        ids = self.ids[:, lanes]
        pieces = []
        for j in range(4):
            at = 512 * p + self.shift + 256 * (j // 2) + 128 * (self.core if j % 2 == 0 else 1 - self.core)
            allowed = line >= ids - at
            if causal:
                allowed = allowed & (line <= self.q_at[:, lanes] - at)
            pieces.append(jnp.where(allowed, s[128 * j : 128 * j + 128, lanes], -1e30))
        masked = jnp.concatenate(pieces, axis=0)
        top = stat_ref[0:1, lanes]
        new_top = jnp.maximum(top, jnp.max(masked, axis=0, keepdims=True))
        expo = jnp.exp2((masked - new_top) * scale)
        fade = jnp.exp2((top - new_top) * scale)
        stat_ref[1:2, lanes] = stat_ref[1:2, lanes] * fade + jnp.sum(expo, axis=0, keepdims=True)
        stat_ref[0:1, lanes] = new_top
        v = jnp.concatenate([ref[2 * p + j, 256:480, :] for j in range(2) for ref in self.refs], axis=1)
        acc_ref[:, lanes] = acc_ref[:, lanes] * fade + jnp.dot(v, expo.astype(bf16), preferred_element_type=f32)

    def back(self, p, low, acc_ref, stat_ref):
        def two(n, carry):
            at = p - 2 * n
            self.score(at - 1, self.odd)
            self.absorb(at, self.even, acc_ref, stat_ref)
            self.score(jnp.maximum(at - 2, 0), self.even)
            self.absorb(at - 1, self.odd, acc_ref, stat_ref)
            return carry

        count = jnp.maximum(p - low + 1, 0)
        lax.fori_loop(0, count >> 1, two, 0)

        @pl.when((count & 1) == 1)
        def _():
            self.absorb(low, self.even, acc_ref, stat_ref)


def own_states(x_ref, rows_ref, keep_ref, maps_ref, send_ref, core):
    total = jnp.zeros((WIDE, STATE), f32)
    for pair in range(4):
        states = []
        for b in (2 * pair, 2 * pair + 1):
            weighted = (x_ref[b].astype(f32) * spread(rows_ref[b, 0:4, :])).astype(bf16)
            state = lax.dot_general(weighted, maps_ref[b, 0:64, :], NT, preferred_element_type=f32)
            states.append(state)
            first, second = spread(keep_ref[b, 0:4, 0:64]), spread(keep_ref[b, 4:8, 0:64])
            total = (first * second) * total + jnp.where(core == 0, second, 1.0) * state
        send_ref[pair] = jnp.concatenate(states, axis=1).astype(bf16)
    return total


def start_all(copies):
    for copy in copies:
        copy.start()


def wait_all(copies):
    for copy in copies:
        copy.wait()


def put_x(x_ref, at, off, acc, total):
    x = (acc / total).astype(bf16)
    for n in range(4):
        x_ref[at + n, pl.ds(off, HEAD_DIM), :] = x[:, 128 * n : 128 * n + 128]


def near_kernel(
    num_any, q_ref, own_ref, other_ref, ds_ref, rows_any, keep_any, maps_any,
    x_out, send_out, left_ref, acc_out, stat_out,
    even, odd, even_2, odd_2, turned, turned_2, acc_ref, stat_ref, x_ref, send_ref, rows_ref, keep_ref, maps_ref, num_ref, sems,
):
    numbers = pltpu.make_async_copy(num_any, num_ref, sems.at[3])
    numbers.start()
    reads = [
        pltpu.make_async_copy(ref.at[pl.ds(8, 8)], to, sems.at[n])
        for n, (ref, to) in enumerate(((rows_any, rows_ref), (keep_any, keep_ref), (maps_any, maps_ref)))
    ]
    start_all(reads)
    acc_ref[...] = jnp.zeros_like(acc_ref)
    stat_ref[...] = jnp.where(iota(stat_ref.shape, 1) == 0, -1e30, 0.0)
    writes = [
        pltpu.make_async_copy(acc_ref.at[pl.ds(0, 2)], acc_out, sems.at[4]),
        pltpu.make_async_copy(stat_ref.at[pl.ds(0, 2)], stat_out, sems.at[5]),
        pltpu.make_async_copy(x_ref, x_out, sems.at[6]),
        pltpu.make_async_copy(send_ref, send_out, sems.at[7]),
    ]
    core = lax.axis_index("core")
    sets = [
        Tiles(core, 0, own_ref, other_ref, q_ref, ds_ref, scratch)
        for scratch in ((even, odd, turned), (even_2, odd_2, turned_2))
    ]
    late = slice(256, 512)

    def state_of(i):
        return acc_ref.at[i], stat_ref.at[i]

    def begin(i):
        tiles = sets[i % 2]
        tiles.start(i)
        tiles.score(2 * i + 1, tiles.odd, late)
        tiles.score(2 * i, tiles.even)

    begin(0)
    for i in range(4):
        if i < 3:
            begin(i + 1)
        tiles = sets[i % 2]
        tiles.absorb(2 * i + 1, tiles.odd, *state_of(i), late, causal=True)
        tiles.absorb(2 * i, tiles.even, *state_of(i), causal=True)
    numbers.wait()
    off = pl.multiple_of(num_ref[OFFSET], 32)
    x_ref[...] = jnp.zeros_like(x_ref)
    for i in range(1, 4):
        tiles = sets[i % 2]
        tiles.start(i)
        tiles.score(2 * i - 1, tiles.even)
        tiles.back(2 * i - 1, jnp.maximum(num_ref[LOW + i], 0), *state_of(i))
        if i == 1:
            start_all(writes[0:2])
        else:
            put_x(x_ref, 4 * i - 8, off, acc_ref[i], stat_ref[i, 1:2, :])
    start_all(writes[2:3])
    wait_all(reads)
    total = own_states(x_ref, rows_ref, keep_ref, maps_ref, send_ref, core)
    start_all(writes[3:4])
    left_ref[...] = jnp.concatenate([total[0:128, :], total[128:256, :]], axis=1).astype(bf16)
    wait_all(writes)


STATE_BUFFERS = [
    pltpu.VMEM((8, 8, ROWS), f32),
    pltpu.VMEM((8, 8, ROWS), f32),
    pltpu.VMEM((8, 128, ROWS), bf16),
]


def attend_near(numbers, q, own, other, ids, rows, keep, maps):
    return pl.pallas_call(
        near_kernel,
        in_specs=[HBM] + [VMEM] * 4 + [HBM] * 3,
        out_specs=(HBM, HBM, VMEM, HBM, HBM),
        out_shape=(
            pltpu.HBM((8, WIDE, ROWS), bf16),
            pltpu.HBM((4, WIDE, 128), bf16),
            jax.ShapeDtypeStruct((128, 128), bf16),
            pltpu.HBM((2, HEAD_DIM, 512), f32),
            pltpu.HBM((2, 8, 512), f32),
        ),
        scratch_shapes=[pltpu.VMEM((512, 512), f32)] * 4
        + [pltpu.VMEM((256, 512), bf16)] * 2
        + [pltpu.VMEM((4, HEAD_DIM, 512), f32), pltpu.VMEM((4, 8, 512), f32)]
        + [pltpu.VMEM((8, WIDE, ROWS), bf16), pltpu.VMEM((4, WIDE, 128), bf16)]
        + STATE_BUFFERS
        + [pltpu.SMEM((NUMBERS,), i32), pltpu.SemaphoreType.DMA((8,))],
        compiler_params=pltpu.CompilerParams(vmem_limit_bytes=VMEM_LIMIT),
        cost_estimate=pl.CostEstimate(flops=5_000_000_000, bytes_accessed=9_000_000, transcendentals=4_000_000),
        name="attend_near",
    )(in_hbm(numbers), q, own, other, ids, in_hbm(rows), in_hbm(keep), in_hbm(maps))


def far_kernel(
    num_any, q_ref, own_ref, other_ref, ds_ref, came_ref, acc_any, stat_any, late_any, rows_any, keep_any, maps_any,
    x_ref, send_ref, even, odd, turned, acc_ref, stat_ref, near_acc, near_stat, rows_ref, keep_ref, maps_ref, num_ref, sems,
):
    reads = [
        pltpu.make_async_copy(num_any, num_ref, sems.at[0]),
        pltpu.make_async_copy(rows_any.at[pl.ds(0, 8)], rows_ref, sems.at[1]),
        pltpu.make_async_copy(keep_any.at[pl.ds(0, 8)], keep_ref, sems.at[2]),
        pltpu.make_async_copy(maps_any.at[pl.ds(0, 8)], maps_ref, sems.at[3]),
    ]
    reads[1:1] = [
        pltpu.make_async_copy(acc_any, near_acc, sems.at[4]),
        pltpu.make_async_copy(stat_any, near_stat, sems.at[5]),
    ]
    reads.append(pltpu.make_async_copy(late_any, send_ref.at[pl.ds(4, 4)], sems.at[6]))
    start_all(reads)
    x_ref[...] = jnp.zeros_like(x_ref)
    send_ref[8, 0:128, :] = came_ref[...]
    send_ref[8, 128:256, :] = jnp.zeros((128, 128), bf16)
    acc_ref[...] = jnp.zeros_like(acc_ref)
    stat_ref[...] = jnp.where(iota(stat_ref.shape, 1) == 0, -1e30, 0.0)
    core = lax.axis_index("core")
    tiles = Tiles(core, -REACH, own_ref, other_ref, q_ref, ds_ref, (even, odd, turned))
    tiles.start(0)
    tiles.score(3, even)
    wait_all(reads[0:1])
    off = pl.multiple_of(num_ref[OFFSET], 32)
    for i in range(2):
        low = jnp.clip(num_ref[LOW + i] + 4, 0, 4)

        @pl.when(low < 4)
        def _():
            if i > 0:
                tiles.start(i)
                tiles.score(3, even)
            tiles.back(3, low, acc_ref.at[i], stat_ref.at[i])

    wait_all(reads[1:3])
    scale = LOG2E / math.sqrt(HEAD_DIM)
    for i in range(2):
        top = jnp.maximum(near_stat[i, 0:1, :], stat_ref[i, 0:1, :])
        near = jnp.exp2((near_stat[i, 0:1, :] - top) * scale)
        far = jnp.exp2((stat_ref[i, 0:1, :] - top) * scale)
        total = near_stat[i, 1:2, :] * near + stat_ref[i, 1:2, :] * far
        put_x(x_ref, 4 * i, off, near_acc[i] * near + acc_ref[i] * far, total)
    wait_all(reads[3:])
    own_states(x_ref, rows_ref, keep_ref, maps_ref, send_ref, core)


def attend_far(numbers, q, own, other, ids, came, acc, stat, rows, keep, maps, late_states):
    return pl.pallas_call(
        far_kernel,
        in_specs=[HBM] + [VMEM] * 5 + [HBM] * 6,
        out_specs=(VMEM,) * 2,
        out_shape=(
            jax.ShapeDtypeStruct((8, WIDE, ROWS), bf16),
            jax.ShapeDtypeStruct((9, WIDE, 128), bf16),
        ),
        scratch_shapes=[pltpu.VMEM((512, 512), f32)] * 2
        + [pltpu.VMEM((256, 512), bf16)]
        + [pltpu.VMEM((2, HEAD_DIM, 512), f32), pltpu.VMEM((2, 8, 512), f32)] * 2
        + STATE_BUFFERS
        + [pltpu.SMEM((NUMBERS,), i32), pltpu.SemaphoreType.DMA((7,))],
        compiler_params=pltpu.CompilerParams(vmem_limit_bytes=VMEM_LIMIT),
        cost_estimate=pl.CostEstimate(flops=2_000_000_000, bytes_accessed=5_000_000, transcendentals=1_000_000),
        name="attend_far",
    )(
        in_hbm(numbers), q, in_vmem(own), other, ids, came, in_hbm(acc), in_hbm(stat), in_hbm(late_states),
        in_hbm(rows), in_hbm(keep), in_hbm(maps),
    )


def scan_kernel(
    num_ref, par_ref, xe_ref, xl_ref, inner_ref, own_ref, other_ref, f_ref, g_ref, rows_ref, keep_ref, bc_ref,
    out_ref, state_ref, hold,
):
    step = pl.program_id(0)
    core, off = num_ref[CORE], pl.multiple_of(num_ref[OFFSET], 32)
    early = step < 2

    @pl.when(step == 0)
    def _():
        packed = f_ref[0, 0:128, :].astype(f32) + g_ref[0, 0:128, :].astype(f32)
        state_ref[0:128, :] = packed[:, 0:64]
        state_ref[128:256, :] = packed[:, 64:128]

    state = state_ref[...]
    for b in range(4):
        at = slice(64 * (b % 2), 64 * (b % 2) + 64)
        mine, theirs = own_ref[b // 2, :, at].astype(f32), other_ref[b // 2, :, at].astype(f32)
        first, second = spread(keep_ref[b, 0:4, 0:64]), spread(keep_ref[b, 4:8, 0:64])
        middle = first * state + jnp.where(core == 0, mine, theirs)
        entering = jnp.where(core == 0, state, middle).astype(bf16)
        state = second * middle + jnp.where(core == 0, theirs, mine)
        carried = jnp.dot(entering, bc_ref[b, 64:128, :], preferred_element_type=f32)
        enter = rows_ref[b, 4:8, :]
        for n in range(SSM):
            rows = slice(64 * n, 64 * n + 64)
            x = jnp.where(early, xe_ref[b, rows, :], xl_ref[b, rows, :])
            y = jnp.dot(x, inner_ref[b, n], preferred_element_type=f32)
            hold[b, rows, :] = y + par_ref[8 + n : 9 + n, :] * x.astype(f32) + carried[rows] * enter[n : n + 1, :]
        out_ref[b] = hold[b, pl.ds(off, HEAD_DIM), :].astype(bf16)
    state_ref[...] = state


def scan(numbers, params, x, inner, own, other, rows, keep, maps):
    def chunks(*shape):
        return pl.BlockSpec(shape, lambda i: (i,) + (0,) * (len(shape) - 1))

    def halves(*shape):
        zeros = (0,) * (len(shape) - 1)
        return [
            pl.BlockSpec(shape, lambda i: (jnp.minimum(i, 1),) + zeros),
            pl.BlockSpec(shape, lambda i: (jnp.maximum(i - 2, 0),) + zeros),
        ]

    return pl.pallas_call(
        scan_kernel,
        grid=(4,),
        in_specs=[SMEM, pl.BlockSpec((16, ROWS), lambda i: (0, 0))]
        + halves(4, WIDE, ROWS)
        + [chunks(4, SSM, ROWS, ROWS)]
        + [chunks(2, WIDE, 128)] * 2
        + [pl.BlockSpec((1, WIDE, 128), lambda i: (8, 0, 0))] * 2
        + [chunks(4, 8, ROWS), chunks(4, 8, ROWS), chunks(4, 128, ROWS)],
        out_specs=chunks(4, HEAD_DIM, ROWS),
        out_shape=jax.ShapeDtypeStruct((CHUNKS, HEAD_DIM, ROWS), bf16),
        scratch_shapes=[pltpu.VMEM((WIDE, STATE), f32), pltpu.VMEM((4, WIDE, ROWS), f32)],
        compiler_params=pltpu.CompilerParams(vmem_limit_bytes=VMEM_LIMIT),
        name="scan",
    )(numbers, params, *x, inner, own, other, own, other, rows, keep, maps)


def other_core(x):
    return lax.ppermute(x, "core", [(0, 1), (1, 0)])


def exchange(x):
    return lax.all_to_all(x, ("y", "x"), split_axis=0, concat_axis=0, tiled=True)


def document_starts(segment_ids, plane):
    padded = jnp.concatenate([jnp.full((REACH + 1,), -1, i32), segment_ids])
    window = lax.dynamic_slice_in_dim(padded, plane * PLANE, PLANE + REACH + 1, 0)
    place = jnp.arange(PLANE + REACH, dtype=i32) - REACH
    starts = jnp.where(window[1:] != window[:-1], place, -REACH).reshape(48, 128)
    within = lax.cummax(starts, axis=1)
    before = lax.cummax(within[:, 127], axis=0)
    before = jnp.concatenate([jnp.full((1,), -REACH, i32), before[:-1]])
    return jnp.maximum(within, before[:, None])[16:]


def on_device(
    queries, keys, values, step_raw, step_bias, decay_rate, skip_gain, state_in, state_out, segment_ids
):
    core, planes = lax.axis_index("core"), lax.axis_size("z")
    plane, head = lax.axis_index("z"), 4 * lax.axis_index("y") + lax.axis_index("x")
    following = [(i, i + 1) for i in range(planes - 1)]

    first = exchange(pack_first(keys, values, jnp.transpose(step_raw), step_bias, decay_rate, skip_gain))
    both = jnp.concatenate([jnp.transpose(state_in), jnp.transpose(state_out)], axis=0).reshape(128, 4, 2, ROWS)
    both = jnp.transpose(lax.dynamic_index_in_dim(both, core, 2, keepdims=False), (1, 0, 2))
    maps = [both] + [lax.ppermute(both, "y", [(i, (i + d) % 4) for i in range(4)]) for d in range(1, 4)]

    starts = document_starts(segment_ids, plane).reshape(CHUNKS, 2, ROWS)
    ids = jnp.where(core == 0, starts, starts[:, ::-1])
    low = ids[0::4, 0, 0] >> 9
    numbers = [core, 32 * (head & 1), lax.axis_index("y"), (7 * head) >> 1]
    numbers = jnp.concatenate([jnp.stack(numbers).astype(i32), low])
    q = jnp.transpose(queries).reshape(HEADS, HEAD_DIM, ROWS)
    first, q = tie(first, q, ids, numbers, *maps)

    q = exchange(q)
    other = other_core(first)
    halo = lax.ppermute(cut(first, other), "z", following)
    inner, rows, params, bc = prep(numbers, first, other, ids, maps)
    keep = keeps(numbers, params, first, other, ids)

    late, late_states, left, acc, stat = attend_near(numbers, q, first, other, ids, rows, keep, bc)
    came = lax.ppermute(left, "z", following)
    halo = gate(halo, late_states)
    early, states = attend_far(
        numbers, q, halo, other_core(halo), ids, came, acc, stat, rows, keep, bc, late_states
    )
    mixed = scan(numbers, params, (early, late), inner, states, other_core(states), rows, keep, bc)
    return jnp.transpose(exchange(mixed).reshape(HEADS * HEAD_DIM, ROWS))


def solution(mesh):
    devices = mesh.devices.reshape(-1, 4, 4, 2)
    return jax.shard_map(
        on_device,
        mesh=Mesh(devices, ("z", "y", "x", "core")),
        in_specs=(
            P(("z", "y", "x", "core"), None),
            P(("z", "y", "x", "core"), None),
            P(("z", "y", "x", "core"), None),
            P(("z", "y", "x", "core"), None),
            P(("x", "core")),
            P(("x", "core")),
            P(("x", "core")),
            P(("z", "y"), None),
            P(("z", "y"), None),
            P(),
        ),
        out_specs=P(("z", "y", "x", "core"), None),
        check_vma=False,
    )
```

```python
import functools
import math

import jax
import jax.numpy as jnp
from jax import lax
from jax.experimental import pallas as pl
from jax.experimental.pallas import tpu as pltpu
from jax.sharding import Mesh
from jax.sharding import PartitionSpec as P

HEADS = 16
HEAD_DIM = 224
SSM_DIM = 64
STATE = 64
ROWS = 128
PLANE = 4096
REACH = 2048
CHUNKS = 16
SSM = 4
WIDE = SSM * SSM_DIM
KV = 480
FIRST = 496
LOG2E = math.log2(math.e)
NT = (((1,), (1,)), ((), ()))
VMEM_LIMIT = 20 * 1024 * 1024

VMEM = pl.BlockSpec(memory_space=pltpu.VMEM)
ANYWHERE = pl.BlockSpec(memory_space=pl.ANY)
SMEM = pl.BlockSpec(memory_space=pltpu.SMEM)
HBM = pl.BlockSpec(memory_space=pltpu.HBM)
CORE, OFFSET, Y_AT, FIRST_MAMBA, LOW = range(5)
NUMBERS = LOW + 4

f32, bf16, i32 = jnp.float32, jnp.bfloat16, jnp.int32


def in_hbm(x):
    return pltpu.with_memory_space_constraint(x, pltpu.HBM)


def in_vmem(x):
    return pltpu.with_memory_space_constraint(x, pltpu.VMEM)


def iota(shape, dim):
    return lax.broadcasted_iota(i32, shape, dim)


def spread(rows):
    width = rows.shape[-1]
    return jnp.concatenate(
        [jnp.broadcast_to(rows[r : r + 1, :], (SSM_DIM, width)) for r in range(SSM)], axis=0
    )


def parts(x):
    high = x.astype(bf16).astype(f32)
    mid = (x - high).astype(bf16).astype(f32)
    return high, mid, x - high - mid


def pack_first_kernel(
    bias_any, decay_any, skip_any, k_any, v_any, raw_any, out_any,
    k_ref, v_ref, raw_ref, out_ref, bias_ref, decay_ref, skip_ref, sems
):
    copies = []
    for step in range(4):
        at = pl.ds(896 * step, 896)
        copies.append(pltpu.make_async_copy(v_any.at[:, at], v_ref.at[step], sems.at[2 * step]))
        copies.append(pltpu.make_async_copy(k_any.at[:, at], k_ref.at[step], sems.at[2 * step + 1]))
    small = [
        pltpu.make_async_copy(have, need, sems.at[12 + n])
        for n, (have, need) in enumerate(
            ((raw_any, raw_ref), (bias_any, bias_ref), (decay_any, decay_ref), (skip_any, skip_ref))
        )
    ]
    start_all(small + copies)
    wait_all(small)
    lane = iota((1, ROWS), 1)
    whole = jnp.zeros((1, ROWS), f32)
    for n, ref in enumerate((bias_ref, decay_ref, skip_ref)):
        for j in range(7):
            whole = jnp.where(lane == 7 * n + j, ref[j], whole)
    high, mid, low = parts(whole)
    rr, jj = iota((256, 56), 0), iota((256, 56), 1)
    chosen = (((rr & 15) < SSM) & (jj == ((7 * (rr >> 4)) >> 1) + (rr & 15))).astype(bf16)
    rows = jnp.dot(chosen, raw_ref[...], preferred_element_type=f32)
    r = iota((256, ROWS), 0) & 15
    rows = jnp.where(r == 4, high, jnp.where(r == 5, mid, jnp.where(r == 6, low, rows))).astype(bf16)
    for h in range(HEADS):
        out_ref[h, 480:496, :] = rows[16 * h : 16 * h + 16, :]
    writes = []
    for step in range(4):
        wait_all(copies[2 * step : 2 * step + 2])
        vt = jnp.transpose(v_ref[step])
        for n in range(4):
            h = 4 * step + n
            k = k_ref[step, :, 224 * n : 224 * n + 224]
            out_ref[h, 0:128, :] = k[:, 0:128]
            out_ref[h, 128:256, :] = jnp.concatenate([k[:, 128:224], jnp.zeros((ROWS, 32), bf16)], axis=1)
            out_ref[h, 256:480, :] = vt[224 * n : 224 * n + 224, :]
        at = pl.ds(4 * step, 4)
        writes.append(pltpu.make_async_copy(out_ref.at[at], out_any.at[at], sems.at[8 + step]))
        writes[-1].start()
    wait_all(writes)


def pack_first(keys, values, raw, step_bias, decay_rate, skip_gain):
    return pl.pallas_call(
        pack_first_kernel,
        in_specs=[HBM] * 6,
        out_specs=HBM,
        out_shape=pltpu.HBM((HEADS, FIRST, ROWS), bf16),
        scratch_shapes=[
            pltpu.VMEM((4, ROWS, 896), bf16),
            pltpu.VMEM((4, ROWS, 896), bf16),
            pltpu.VMEM((56, ROWS), bf16),
            pltpu.VMEM((HEADS, FIRST, ROWS), bf16),
            pltpu.SMEM((7,), f32),
            pltpu.SMEM((7,), f32),
            pltpu.SMEM((7,), f32),
            pltpu.SemaphoreType.DMA((16,)),
        ],
        compiler_params=pltpu.CompilerParams(vmem_limit_bytes=VMEM_LIMIT),
        name="pack_keys_values",
    )(*(in_hbm(x) for x in (step_bias, decay_rate, skip_gain, keys, values, raw)))


def cut_kernel(first_ref, before_ref, out_ref):
    out_ref[...] = first_ref[8:16, 0:KV, :]


def cut(first, before):
    return pl.pallas_call(
        cut_kernel,
        in_specs=[VMEM, ANYWHERE],
        out_specs=VMEM,
        out_shape=jax.ShapeDtypeStruct((8, KV, ROWS), bf16),
        compiler_params=pltpu.CompilerParams(vmem_limit_bytes=VMEM_LIMIT),
        name="cut_halo",
    )(first, before)


def gate_kernel(*refs):
    pass


def gate(x, *before):
    return pl.pallas_call(
        gate_kernel,
        in_specs=[ANYWHERE] * (1 + len(before)),
        out_specs=ANYWHERE,
        out_shape=pltpu.VMEM(x.shape, x.dtype),
        input_output_aliases={0: 0},
        name="gate",
    )(in_vmem(x), *before)


def tie(first, q, *before):
    return pl.pallas_call(
        gate_kernel,
        in_specs=[ANYWHERE] * (2 + len(before)),
        out_specs=(ANYWHERE,) * 2,
        out_shape=(pltpu.VMEM(first.shape, first.dtype), jax.ShapeDtypeStruct(q.shape, q.dtype)),
        input_output_aliases={0: 0, 1: 1},
        name="tie",
    )(in_vmem(first), q, *before)


def step_sizes(raw, bias, decay):
    z = raw + bias
    dt = jnp.maximum(z, 0.0) + jnp.log1p(jnp.exp(-jnp.abs(z)))
    return dt, -dt * decay


def prep_kernel(
    num_ref, own_ref, other_ref, ds_ref, b0_ref, b1_ref, b2_ref, b3_ref, inner_out, rows_out, par_ref, bc_out,
    inner_ref, rows_ref, bc_ref, sems,
):
    core = num_ref[CORE]
    copies = [
        pltpu.make_async_copy(ref, bc_ref.at[pl.ds(4 * ((num_ref[Y_AT] - d) & 3), 4)], sems.at[d])
        for d, ref in enumerate((b0_ref, b1_ref, b2_ref, b3_ref))
    ]
    for copy in copies:
        copy.start()
    shape = (CHUNKS * 16, ROWS)
    line, lane = iota(shape, 0), iota(shape, 1)
    r = line & 15
    bias, decay = jnp.zeros(shape, f32), jnp.zeros(shape, f32)
    par_ref[...] = jnp.zeros_like(par_ref)
    for n in range(SSM):
        mamba = num_ref[FIRST_MAMBA] + n
        holder = (mamba * 37) >> 8
        at = mamba - 7 * holder
        held = jnp.where((holder & 1) == core, own_ref[holder >> 1], other_ref[holder >> 1]).astype(f32)
        held = held[4:5, :] + held[5:6, :] + held[6:7, :]

        def value(which):
            chosen = jnp.where(iota((1, ROWS), 1) == 7 * which + at, held, 0.0)
            return jnp.sum(chosen, axis=1, keepdims=True)

        for which in range(3):
            par_ref[4 * which + n : 4 * which + n + 1, :] = jnp.broadcast_to(value(which), (1, ROWS))
        bias = jnp.where(r == n, value(0), bias)
        decay = jnp.where(r == n, value(1), decay)
    upper = (iota((ROWS, ROWS), 0) <= iota((ROWS, ROWS), 1)).astype(f32)
    ids = spread_ids(ds_ref, 0)
    dt, log_step = step_sizes(own_ref[...].reshape(shape).astype(f32), bias, decay)
    running = jnp.dot(log_step, upper, precision=lax.Precision.HIGHEST, preferred_element_type=f32)
    start = 256 * (line >> 4) + 128 * core
    whole = jnp.broadcast_to(running[:, 127:128], shape)
    last = jnp.broadcast_to(ids[:, 127:128], shape)
    tail = jnp.where(start + lane >= last, jnp.exp(whole - running) * dt, 0.0)
    enter = jnp.where(ids < start, jnp.exp(running), 0.0)
    for b in range(CHUNKS):
        at = 16 * b
        rows_ref[b, 0:4, :] = tail[at : at + 4, :]
        rows_ref[b, 4:8, :] = enter[at : at + 4, :]
    writes = [pltpu.make_async_copy(rows_ref, rows_out, sems.at[4])]
    writes[0].start()
    running_t, dt_t = jnp.transpose(running), jnp.transpose(dt)
    s_at, t_at = iota((ROWS, ROWS), 0), iota((ROWS, ROWS), 1)
    wait_all(copies)
    writes.append(pltpu.make_async_copy(bc_ref, bc_out, sems.at[5]))
    writes[1].start()
    for b in range(CHUNKS):
        at = 16 * b
        state_in = jnp.transpose(bc_ref[b, 0:64, :].astype(f32)).astype(bf16)
        mix = jnp.dot(state_in, bc_ref[b, 64:128, :], preferred_element_type=f32)
        base = 256 * b + 128 * core
        allowed = (s_at <= t_at) & (s_at >= ids[at : at + 1, :] - base)
        for n in range(SSM):
            gap = running[at + n : at + n + 1, :] - running_t[:, at + n : at + n + 1]
            value = jnp.exp(jnp.where(allowed, gap, 0.0)) * mix * dt_t[:, at + n : at + n + 1]
            inner_ref[b, n, :, :] = jnp.where(allowed, value, 0.0).astype(bf16)
        writes.append(pltpu.make_async_copy(inner_ref.at[b], inner_out.at[b], sems.at[6 + b]))
        writes[-1].start()
    wait_all(writes)


def spread_ids(ds_ref, which):
    return jnp.concatenate(
        [jnp.broadcast_to(ds_ref[b, which : which + 1, :], (16, ROWS)) for b in range(CHUNKS)], axis=0
    )


STEPS = pl.BlockSpec((CHUNKS, 16, ROWS), lambda i: (0, 30, 0))


def prep(numbers, own, other, ids, maps):
    return pl.pallas_call(
        prep_kernel,
        grid=(1,),
        in_specs=[SMEM, STEPS, STEPS, VMEM] + [ANYWHERE] * 4,
        out_shape=(
            pltpu.HBM((CHUNKS, SSM, ROWS, ROWS), bf16),
            pltpu.HBM((CHUNKS, 8, ROWS), f32),
            jax.ShapeDtypeStruct((16, ROWS), f32),
            pltpu.HBM((CHUNKS, 128, ROWS), bf16),
        ),
        out_specs=(HBM, HBM, VMEM, HBM),
        scratch_shapes=[
            pltpu.VMEM((CHUNKS, SSM, ROWS, ROWS), bf16),
            pltpu.VMEM((CHUNKS, 8, ROWS), f32),
            pltpu.VMEM((CHUNKS, 128, ROWS), bf16),
            pltpu.SemaphoreType.DMA((6 + CHUNKS,)),
        ],
        compiler_params=pltpu.CompilerParams(vmem_limit_bytes=VMEM_LIMIT),
        cost_estimate=pl.CostEstimate(flops=200_000_000, bytes_accessed=8_000_000, transcendentals=2_000_000),
        name="scan_weights",
    )(numbers, own, other, ids, *maps)


def keep_kernel(num_ref, par_ref, own_ref, other_ref, ds_ref, keep_ref):
    core = num_ref[CORE]
    shape = (CHUNKS * 16, ROWS)
    line = iota(shape, 0)
    bias = jnp.concatenate([par_ref[0:4, :], jnp.zeros((12, ROWS), f32)] * CHUNKS, axis=0)
    decay = jnp.concatenate([par_ref[4:8, :], jnp.zeros((12, ROWS), f32)] * CHUNKS, axis=0)

    def keep(which):
        at = jnp.where(which == core, 0, 1)
        ids = jnp.where(at == 0, spread_ids(ds_ref, 0), spread_ids(ds_ref, 1))
        raw = jnp.where(at == 0, own_ref[...], other_ref[...]).reshape(shape).astype(f32)
        whole = jnp.sum(step_sizes(raw, bias, decay)[1], axis=1, keepdims=True)
        value = jnp.where(ids[:, 127:128] < 256 * (line[:, 0:1] >> 4) + 128 * which, jnp.exp(whole), 0.0)
        return jnp.broadcast_to(value, shape)

    for which in range(2):
        kept = keep(which)
        for b in range(CHUNKS):
            keep_ref[b, 4 * which : 4 * which + 4, :] = kept[16 * b : 16 * b + 4, :]


def keeps(numbers, params, own, other, ids):
    return pl.pallas_call(
        keep_kernel,
        grid=(1,),
        in_specs=[SMEM, VMEM, STEPS, STEPS, VMEM],
        out_specs=VMEM,
        out_shape=jax.ShapeDtypeStruct((CHUNKS, 8, ROWS), f32),
        compiler_params=pltpu.CompilerParams(vmem_limit_bytes=VMEM_LIMIT),
        name="scan_keeps",
    )(numbers, params, own, other, ids)


class Tiles:
    def __init__(self, core, shift, own, other, q, ds, scratch):
        self.core, self.shift, self.refs, self.q, self.ds = core, shift, (own, other), q, ds
        self.even, self.odd, self.turned = scratch

    def start(self, tile):
        for n in range(4):
            self.turned[0:HEAD_DIM, 128 * n : 128 * n + 128] = self.q[4 * tile + n]
        self.turned[HEAD_DIM:256, :] = jnp.zeros((32, 512), bf16)
        self.ids = jnp.concatenate([self.ds[4 * tile + n, 0:1, :] for n in range(4)], axis=1)
        lane = iota((1, 512), 1)
        self.q_at = 1024 * tile + 128 * self.core + (lane & 127) + 256 * (lane >> 7)

    def score(self, p, s, lanes=slice(0, 512)):
        k = jnp.concatenate(
            [
                jnp.concatenate([ref[2 * p + j, 0:128, :], ref[2 * p + j, 128:256, :]], axis=1)
                for j in range(2)
                for ref in self.refs
            ],
            axis=0,
        )
        s[:, lanes] = jnp.dot(k, self.turned[:, lanes], preferred_element_type=f32)

    def absorb(self, p, s, acc_ref, stat_ref, lanes=slice(0, 512), causal=False):
        width = lanes.stop - lanes.start
        scale = LOG2E / math.sqrt(HEAD_DIM)
        line = iota((ROWS, width), 0)
        ids = self.ids[:, lanes]
        pieces = []
        for j in range(4):
            at = 512 * p + self.shift + 256 * (j // 2) + 128 * (self.core if j % 2 == 0 else 1 - self.core)
            allowed = line >= ids - at
            if causal:
                allowed = allowed & (line <= self.q_at[:, lanes] - at)
            pieces.append(jnp.where(allowed, s[128 * j : 128 * j + 128, lanes], -1e30))
        masked = jnp.concatenate(pieces, axis=0)
        top = stat_ref[0:1, lanes]
        new_top = jnp.maximum(top, jnp.max(masked, axis=0, keepdims=True))
        expo = jnp.exp2((masked - new_top) * scale)
        fade = jnp.exp2((top - new_top) * scale)
        stat_ref[1:2, lanes] = stat_ref[1:2, lanes] * fade + jnp.sum(expo, axis=0, keepdims=True)
        stat_ref[0:1, lanes] = new_top
        v = jnp.concatenate([ref[2 * p + j, 256:480, :] for j in range(2) for ref in self.refs], axis=1)
        acc_ref[:, lanes] = acc_ref[:, lanes] * fade + jnp.dot(v, expo.astype(bf16), preferred_element_type=f32)

    def back(self, p, low, acc_ref, stat_ref):
        def two(n, carry):
            at = p - 2 * n
            self.score(at - 1, self.odd)
            self.absorb(at, self.even, acc_ref, stat_ref)
            self.score(jnp.maximum(at - 2, 0), self.even)
            self.absorb(at - 1, self.odd, acc_ref, stat_ref)
            return carry

        count = jnp.maximum(p - low + 1, 0)
        lax.fori_loop(0, count >> 1, two, 0)

        @pl.when((count & 1) == 1)
        def _():
            self.absorb(low, self.even, acc_ref, stat_ref)


def own_states(x_ref, rows_ref, keep_ref, maps_ref, send_ref, core):
    total = jnp.zeros((WIDE, STATE), f32)
    for pair in range(4):
        states = []
        for b in (2 * pair, 2 * pair + 1):
            weighted = (x_ref[b].astype(f32) * spread(rows_ref[b, 0:4, :])).astype(bf16)
            state = lax.dot_general(weighted, maps_ref[b, 0:64, :], NT, preferred_element_type=f32)
            states.append(state)
            first, second = spread(keep_ref[b, 0:4, 0:64]), spread(keep_ref[b, 4:8, 0:64])
            total = (first * second) * total + jnp.where(core == 0, second, 1.0) * state
        send_ref[pair] = jnp.concatenate(states, axis=1).astype(bf16)
    return total


def start_all(copies):
    for copy in copies:
        copy.start()


def wait_all(copies):
    for copy in copies:
        copy.wait()


def put_x(x_ref, at, off, acc, total):
    x = (acc / total).astype(bf16)
    for n in range(4):
        x_ref[at + n, pl.ds(off, HEAD_DIM), :] = x[:, 128 * n : 128 * n + 128]


def near_kernel(
    num_any, q_ref, own_ref, other_ref, ds_ref, rows_any, keep_any, maps_any,
    x_out, send_out, left_ref, acc_out, stat_out,
    even, odd, even_2, odd_2, turned, turned_2, acc_ref, stat_ref, x_ref, send_ref, rows_ref, keep_ref, maps_ref, num_ref, sems,
):
    numbers = pltpu.make_async_copy(num_any, num_ref, sems.at[3])
    numbers.start()
    reads = [
        pltpu.make_async_copy(ref.at[pl.ds(8, 8)], to, sems.at[n])
        for n, (ref, to) in enumerate(((rows_any, rows_ref), (keep_any, keep_ref), (maps_any, maps_ref)))
    ]
    start_all(reads)
    acc_ref[...] = jnp.zeros_like(acc_ref)
    stat_ref[...] = jnp.where(iota(stat_ref.shape, 1) == 0, -1e30, 0.0)
    writes = [
        pltpu.make_async_copy(acc_ref.at[pl.ds(0, 2)], acc_out, sems.at[4]),
        pltpu.make_async_copy(stat_ref.at[pl.ds(0, 2)], stat_out, sems.at[5]),
        pltpu.make_async_copy(x_ref, x_out, sems.at[6]),
        pltpu.make_async_copy(send_ref, send_out, sems.at[7]),
    ]
    core = lax.axis_index("core")
    sets = [
        Tiles(core, 0, own_ref, other_ref, q_ref, ds_ref, scratch)
        for scratch in ((even, odd, turned), (even_2, odd_2, turned_2))
    ]
    late = slice(256, 512)

    def state_of(i):
        return acc_ref.at[i], stat_ref.at[i]

    def begin(i):
        tiles = sets[i % 2]
        tiles.start(i)
        tiles.score(2 * i + 1, tiles.odd, late)
        tiles.score(2 * i, tiles.even)

    begin(0)
    for i in range(4):
        if i < 3:
            begin(i + 1)
        tiles = sets[i % 2]
        tiles.absorb(2 * i + 1, tiles.odd, *state_of(i), late, causal=True)
        tiles.absorb(2 * i, tiles.even, *state_of(i), causal=True)
    numbers.wait()
    off = pl.multiple_of(num_ref[OFFSET], 32)
    x_ref[...] = jnp.zeros_like(x_ref)
    for i in range(1, 4):
        tiles = sets[i % 2]
        tiles.start(i)
        tiles.score(2 * i - 1, tiles.even)
        tiles.back(2 * i - 1, jnp.maximum(num_ref[LOW + i], 0), *state_of(i))
        if i == 1:
            start_all(writes[0:2])
        else:
            put_x(x_ref, 4 * i - 8, off, acc_ref[i], stat_ref[i, 1:2, :])
    start_all(writes[2:3])
    wait_all(reads)
    total = own_states(x_ref, rows_ref, keep_ref, maps_ref, send_ref, core)
    start_all(writes[3:4])
    left_ref[...] = jnp.concatenate([total[0:128, :], total[128:256, :]], axis=1).astype(bf16)
    wait_all(writes)


STATE_BUFFERS = [
    pltpu.VMEM((8, 8, ROWS), f32),
    pltpu.VMEM((8, 8, ROWS), f32),
    pltpu.VMEM((8, 128, ROWS), bf16),
]


def attend_near(numbers, q, own, other, ids, rows, keep, maps):
    return pl.pallas_call(
        near_kernel,
        in_specs=[HBM] + [VMEM] * 4 + [HBM] * 3,
        out_specs=(HBM, HBM, VMEM, HBM, HBM),
        out_shape=(
            pltpu.HBM((8, WIDE, ROWS), bf16),
            pltpu.HBM((4, WIDE, 128), bf16),
            jax.ShapeDtypeStruct((128, 128), bf16),
            pltpu.HBM((2, HEAD_DIM, 512), f32),
            pltpu.HBM((2, 8, 512), f32),
        ),
        scratch_shapes=[pltpu.VMEM((512, 512), f32)] * 4
        + [pltpu.VMEM((256, 512), bf16)] * 2
        + [pltpu.VMEM((4, HEAD_DIM, 512), f32), pltpu.VMEM((4, 8, 512), f32)]
        + [pltpu.VMEM((8, WIDE, ROWS), bf16), pltpu.VMEM((4, WIDE, 128), bf16)]
        + STATE_BUFFERS
        + [pltpu.SMEM((NUMBERS,), i32), pltpu.SemaphoreType.DMA((8,))],
        compiler_params=pltpu.CompilerParams(vmem_limit_bytes=VMEM_LIMIT),
        cost_estimate=pl.CostEstimate(flops=5_000_000_000, bytes_accessed=9_000_000, transcendentals=4_000_000),
        name="attend_near",
    )(in_hbm(numbers), q, own, other, ids, in_hbm(rows), in_hbm(keep), in_hbm(maps))


def far_kernel(
    num_any, q_ref, own_ref, other_ref, ds_ref, came_ref, acc_any, stat_any, late_any, rows_any, keep_any, maps_any,
    x_ref, send_ref, even, odd, turned, acc_ref, stat_ref, near_acc, near_stat, rows_ref, keep_ref, maps_ref, num_ref, sems,
):
    reads = [
        pltpu.make_async_copy(num_any, num_ref, sems.at[0]),
        pltpu.make_async_copy(rows_any.at[pl.ds(0, 8)], rows_ref, sems.at[1]),
        pltpu.make_async_copy(keep_any.at[pl.ds(0, 8)], keep_ref, sems.at[2]),
        pltpu.make_async_copy(maps_any.at[pl.ds(0, 8)], maps_ref, sems.at[3]),
    ]
    reads[1:1] = [
        pltpu.make_async_copy(acc_any, near_acc, sems.at[4]),
        pltpu.make_async_copy(stat_any, near_stat, sems.at[5]),
    ]
    reads.append(pltpu.make_async_copy(late_any, send_ref.at[pl.ds(4, 4)], sems.at[6]))
    start_all(reads)
    x_ref[...] = jnp.zeros_like(x_ref)
    send_ref[8, 0:128, :] = came_ref[...]
    send_ref[8, 128:256, :] = jnp.zeros((128, 128), bf16)
    acc_ref[...] = jnp.zeros_like(acc_ref)
    stat_ref[...] = jnp.where(iota(stat_ref.shape, 1) == 0, -1e30, 0.0)
    core = lax.axis_index("core")
    tiles = Tiles(core, -REACH, own_ref, other_ref, q_ref, ds_ref, (even, odd, turned))
    tiles.start(0)
    tiles.score(3, even)
    wait_all(reads[0:1])
    off = pl.multiple_of(num_ref[OFFSET], 32)
    for i in range(2):
        low = jnp.clip(num_ref[LOW + i] + 4, 0, 4)

        @pl.when(low < 4)
        def _():
            if i > 0:
                tiles.start(i)
                tiles.score(3, even)
            tiles.back(3, low, acc_ref.at[i], stat_ref.at[i])

    wait_all(reads[1:3])
    scale = LOG2E / math.sqrt(HEAD_DIM)
    for i in range(2):
        top = jnp.maximum(near_stat[i, 0:1, :], stat_ref[i, 0:1, :])
        near = jnp.exp2((near_stat[i, 0:1, :] - top) * scale)
        far = jnp.exp2((stat_ref[i, 0:1, :] - top) * scale)
        total = near_stat[i, 1:2, :] * near + stat_ref[i, 1:2, :] * far
        put_x(x_ref, 4 * i, off, near_acc[i] * near + acc_ref[i] * far, total)
    wait_all(reads[3:])
    own_states(x_ref, rows_ref, keep_ref, maps_ref, send_ref, core)


def attend_far(numbers, q, own, other, ids, came, acc, stat, rows, keep, maps, late_states):
    return pl.pallas_call(
        far_kernel,
        in_specs=[HBM] + [VMEM] * 5 + [HBM] * 6,
        out_specs=(VMEM,) * 2,
        out_shape=(
            jax.ShapeDtypeStruct((8, WIDE, ROWS), bf16),
            jax.ShapeDtypeStruct((9, WIDE, 128), bf16),
        ),
        scratch_shapes=[pltpu.VMEM((512, 512), f32)] * 2
        + [pltpu.VMEM((256, 512), bf16)]
        + [pltpu.VMEM((2, HEAD_DIM, 512), f32), pltpu.VMEM((2, 8, 512), f32)] * 2
        + STATE_BUFFERS
        + [pltpu.SMEM((NUMBERS,), i32), pltpu.SemaphoreType.DMA((7,))],
        compiler_params=pltpu.CompilerParams(vmem_limit_bytes=VMEM_LIMIT),
        cost_estimate=pl.CostEstimate(flops=2_000_000_000, bytes_accessed=5_000_000, transcendentals=1_000_000),
        name="attend_far",
    )(
        in_hbm(numbers), q, in_vmem(own), other, ids, came, in_hbm(acc), in_hbm(stat), in_hbm(late_states),
        in_hbm(rows), in_hbm(keep), in_hbm(maps),
    )


def scan_kernel(
    num_ref, par_ref, xe_ref, xl_ref, inner_ref, own_ref, other_ref, f_ref, g_ref, rows_ref, keep_ref, bc_ref,
    out_ref, state_ref, hold,
):
    step = pl.program_id(0)
    core, off = num_ref[CORE], pl.multiple_of(num_ref[OFFSET], 32)
    early = step < 2

    @pl.when(step == 0)
    def _():
        packed = f_ref[0, 0:128, :].astype(f32) + g_ref[0, 0:128, :].astype(f32)
        state_ref[0:128, :] = packed[:, 0:64]
        state_ref[128:256, :] = packed[:, 64:128]

    state = state_ref[...]
    for b in range(4):
        at = slice(64 * (b % 2), 64 * (b % 2) + 64)
        mine, theirs = own_ref[b // 2, :, at].astype(f32), other_ref[b // 2, :, at].astype(f32)
        first, second = spread(keep_ref[b, 0:4, 0:64]), spread(keep_ref[b, 4:8, 0:64])
        middle = first * state + jnp.where(core == 0, mine, theirs)
        entering = jnp.where(core == 0, state, middle).astype(bf16)
        state = second * middle + jnp.where(core == 0, theirs, mine)
        carried = jnp.dot(entering, bc_ref[b, 64:128, :], preferred_element_type=f32)
        enter = rows_ref[b, 4:8, :]
        for n in range(SSM):
            rows = slice(64 * n, 64 * n + 64)
            x = jnp.where(early, xe_ref[b, rows, :], xl_ref[b, rows, :])
            y = jnp.dot(x, inner_ref[b, n], preferred_element_type=f32)
            hold[b, rows, :] = y + par_ref[8 + n : 9 + n, :] * x.astype(f32) + carried[rows] * enter[n : n + 1, :]
        out_ref[b] = hold[b, pl.ds(off, HEAD_DIM), :].astype(bf16)
    state_ref[...] = state


def scan(numbers, params, x, inner, own, other, rows, keep, maps):
    def chunks(*shape):
        return pl.BlockSpec(shape, lambda i: (i,) + (0,) * (len(shape) - 1))

    def halves(*shape):
        zeros = (0,) * (len(shape) - 1)
        return [
            pl.BlockSpec(shape, lambda i: (jnp.minimum(i, 1),) + zeros),
            pl.BlockSpec(shape, lambda i: (jnp.maximum(i - 2, 0),) + zeros),
        ]

    return pl.pallas_call(
        scan_kernel,
        grid=(4,),
        in_specs=[SMEM, pl.BlockSpec((16, ROWS), lambda i: (0, 0))]
        + halves(4, WIDE, ROWS)
        + [chunks(4, SSM, ROWS, ROWS)]
        + [chunks(2, WIDE, 128)] * 2
        + [pl.BlockSpec((1, WIDE, 128), lambda i: (8, 0, 0))] * 2
        + [chunks(4, 8, ROWS), chunks(4, 8, ROWS), chunks(4, 128, ROWS)],
        out_specs=chunks(4, HEAD_DIM, ROWS),
        out_shape=jax.ShapeDtypeStruct((CHUNKS, HEAD_DIM, ROWS), bf16),
        scratch_shapes=[pltpu.VMEM((WIDE, STATE), f32), pltpu.VMEM((4, WIDE, ROWS), f32)],
        compiler_params=pltpu.CompilerParams(vmem_limit_bytes=VMEM_LIMIT),
        name="scan",
    )(numbers, params, *x, inner, own, other, own, other, rows, keep, maps)


def other_core(x):
    return lax.ppermute(x, "core", [(0, 1), (1, 0)])


def exchange(x):
    return lax.all_to_all(x, ("y", "x"), split_axis=0, concat_axis=0, tiled=True)


def document_starts(segment_ids, plane):
    padded = jnp.concatenate([jnp.full((REACH + 1,), -1, i32), segment_ids])
    window = lax.dynamic_slice_in_dim(padded, plane * PLANE, PLANE + REACH + 1, 0)
    place = jnp.arange(PLANE + REACH, dtype=i32) - REACH
    starts = jnp.where(window[1:] != window[:-1], place, -REACH).reshape(48, 128)
    within = lax.cummax(starts, axis=1)
    before = lax.cummax(within[:, 127], axis=0)
    before = jnp.concatenate([jnp.full((1,), -REACH, i32), before[:-1]])
    return jnp.maximum(within, before[:, None])[16:]


def on_device(
    queries, keys, values, step_raw, step_bias, decay_rate, skip_gain, state_in, state_out, segment_ids
):
    core, planes = lax.axis_index("core"), lax.axis_size("z")
    plane, head = lax.axis_index("z"), 4 * lax.axis_index("y") + lax.axis_index("x")
    following = [(i, i + 1) for i in range(planes - 1)]

    first = exchange(pack_first(keys, values, jnp.transpose(step_raw), step_bias, decay_rate, skip_gain))
    both = jnp.concatenate([jnp.transpose(state_in), jnp.transpose(state_out)], axis=0).reshape(128, 4, 2, ROWS)
    both = jnp.transpose(lax.dynamic_index_in_dim(both, core, 2, keepdims=False), (1, 0, 2))
    maps = [both] + [lax.ppermute(both, "y", [(i, (i + d) % 4) for i in range(4)]) for d in range(1, 4)]

    starts = document_starts(segment_ids, plane).reshape(CHUNKS, 2, ROWS)
    ids = jnp.where(core == 0, starts, starts[:, ::-1])
    low = ids[0::4, 0, 0] >> 9
    numbers = [core, 32 * (head & 1), lax.axis_index("y"), (7 * head) >> 1]
    numbers = jnp.concatenate([jnp.stack(numbers).astype(i32), low])
    q = jnp.transpose(queries).reshape(HEADS, HEAD_DIM, ROWS)
    first, q = tie(first, q, ids, numbers, *maps)

    q = exchange(q)
    other = other_core(first)
    halo = lax.ppermute(cut(first, other), "z", following)
    inner, rows, params, bc = prep(numbers, first, other, ids, maps)
    keep = keeps(numbers, params, first, other, ids)

    late, late_states, left, acc, stat = attend_near(numbers, q, first, other, ids, rows, keep, bc)
    came = lax.ppermute(left, "z", following)
    halo = gate(halo, late_states)
    early, states = attend_far(
        numbers, q, halo, other_core(halo), ids, came, acc, stat, rows, keep, bc, late_states
    )
    mixed = scan(numbers, params, (early, late), inner, states, other_core(states), rows, keep, bc)
    return jnp.transpose(exchange(mixed).reshape(HEADS * HEAD_DIM, ROWS))


def solution(mesh):
    devices = mesh.devices.reshape(-1, 4, 4, 2)
    return jax.shard_map(
        on_device,
        mesh=Mesh(devices, ("z", "y", "x", "core")),
        in_specs=(
            P(("z", "y", "x", "core"), None),
            P(("z", "y", "x", "core"), None),
            P(("z", "y", "x", "core"), None),
            P(("z", "y", "x", "core"), None),
            P(("x", "core")),
            P(("x", "core")),
            P(("x", "core")),
            P(("z", "y"), None),
            P(("z", "y"), None),
            P(),
        ),
        out_specs=P(("z", "y", "x", "core"), None),
        check_vma=False,
    )
```
